32 devices in a mesh: dp: 4 (over z), ctx: 8 (over y, x, core).
Axes of the slice: x: 2, y: 2, z: 4, core: 2. Of those that a mesh axis runs over, the one named last changes fastest.
Arguments:
- frames: bfloat16 [4, 1024, 512], P('dp', 'ctx'), may hold values from -6 to 6
- conv_weight: bfloat16 [3, 512, 512], replicated, may hold values from -0.15625 to 0.15625
- proj_weight: bfloat16 [512, 768], replicated, may hold values from -0.25 to 0.25
- query_weight: bfloat16 [768, 384], replicated, may hold values from -1.5 to 1.5
- key_weight: bfloat16 [768, 384], replicated, may hold values from -1.5 to 1.5
- value_weight: bfloat16 [768, 384], replicated, may hold values from -0.21875 to 0.21875
- cotangent: bfloat16 [4, 512, 384], P('dp', 'ctx'), may hold values from -6 to 6
Outputs:
- weight_grad: float32 [1536, 512], P('ctx', 'dp')
- frame_grad: bfloat16 [4, 1024, 512], P('dp', 'ctx')
The draws below stay inside these ranges and needn't reach their ends.
All inputs are finite; a program needn't handle non-finite values.
Results may differ from the reference program's by a relative error of at most 0.04.
Values may be sent and summed in bfloat16 or wider, within the bound.
A program may use at most 64 MiB of HBM per device.

```python
import jax
import jax.numpy as jnp
from jax import lax

C = 512
D = 768
HEADS = 6
HEAD_DIM = 64
HD = 384
LENGTH = 512
RECORDS = 4


def draw_query_weight(key, part):
    own_part = jax.random.normal(jax.random.fold_in(key, 7), (D, HD), jnp.float32)
    result = 1.8 * own_part * D ** (-0.5)
    return jnp.clip(result, -1.5, 1.5).astype(jnp.bfloat16)


def draw_key_weight(key, part):
    own_part = jax.random.normal(jax.random.fold_in(key, 11), (D, HD), jnp.float32)
    result = 1.8 * own_part * D ** (-0.5)
    return jnp.clip(result, -1.5, 1.5).astype(jnp.bfloat16)


def block_levels(own_key, extent, cuts, smallest, largest):
    def one(position, blocks):
        draws = jax.random.uniform(jax.random.fold_in(jax.random.fold_in(own_key, 6), position), (blocks,), jnp.float32, smallest / len(cuts), largest / len(cuts))
        return jnp.repeat(jnp.exp(draws), extent[position] // blocks).reshape((-1,) + (1,) * (len(extent) - position - 1))

    loudness = one(*cuts[0])
    for cut in cuts[1:]:
        loudness = loudness * one(*cut)
    return loudness


def normal_values(rng, shape, width, bound, shards=(), held_as=jnp.bfloat16):
    level = block_levels(rng, shape, shards, -0.22, 0.18) if shards else 1.0
    array = jax.random.normal(rng, shape, jnp.float32) * width * level
    return jnp.minimum(jnp.maximum(array, -bound), bound).astype(held_as)


def setup_inputs(seed: int = 0) -> dict:
    splits = jax.random.split(jax.random.key(seed), 8)
    frames = normal_values(splits[0], (RECORDS, 2 * LENGTH, C), 1.0, 6.0, ((0, 4), (1, 8)))
    conv_weight = normal_values(splits[1], (3, C, C), (3 * C) ** -0.5, 0.15625)
    proj_weight = normal_values(splits[2], (C, D), C ** -0.5, 0.25)
    query_weight = draw_query_weight(jax.random.fold_in(splits[7], 71), 0)
    key_weight = draw_key_weight(jax.random.fold_in(splits[7], 71), 0)
    value_weight = normal_values(splits[5], (D, HD), D ** -0.5, 0.21875)
    cotangent = normal_values(splits[6], (RECORDS, LENGTH, HD), 1.0, 6.0, ((0, 4), (1, 8)))
    return {"frames": frames, "conv_weight": conv_weight, "proj_weight": proj_weight, "query_weight": query_weight, "key_weight": key_weight, "value_weight": value_weight, "cotangent": cotangent}


SQRT_HALF = 0.7071067811865476
INV_ROOT_TAU = 0.3989422804014327
EPSILON = 1e-05

def lowered(value):
    return lax.optimization_barrier(value.astype(jnp.bfloat16)).astype(jnp.float32)

def gelu_slope(pre):
    return 0.5 * (1.0 + lax.erf(pre * SQRT_HALF)) + pre * INV_ROOT_TAU * jnp.exp(-0.5 * pre * pre)

def one_record(frames_rec, cot_rec, conv_weight, proj_weight, query_weight, key_weight, value_weight):
    length = cot_rec.shape[0]
    padded = jnp.concatenate([frames_rec, jnp.zeros((1, C), frames_rec.dtype)], 0)
    taps = [padded[offset:offset + 2 * length:2] for offset in range(3)]
    conv_out = jnp.dot(taps[0], conv_weight[0], preferred_element_type=jnp.float32)
    conv_out = conv_out + jnp.dot(taps[1], conv_weight[1], preferred_element_type=jnp.float32)
    conv_out = conv_out + jnp.dot(taps[2], conv_weight[2], preferred_element_type=jnp.float32)
    activated = jax.nn.gelu(conv_out, approximate=False)
    centre = lax.optimization_barrier(jnp.mean(activated, -1, keepdims=True))
    spread = lax.optimization_barrier(jnp.mean((activated - centre) ** 2, -1, keepdims=True))
    inv_std = lax.rsqrt(spread + EPSILON)
    normed = (activated - centre) * inv_std
    hidden = jnp.dot(normed.astype(jnp.bfloat16), proj_weight, preferred_element_type=jnp.float32).astype(jnp.bfloat16)
    queries = jnp.dot(hidden, query_weight, preferred_element_type=jnp.float32).astype(jnp.bfloat16)
    keys = jnp.dot(hidden, key_weight, preferred_element_type=jnp.float32).astype(jnp.bfloat16)
    values = jnp.dot(hidden, value_weight, preferred_element_type=jnp.float32).astype(jnp.bfloat16)
    scale = HEAD_DIM ** (-0.5)
    query_f = queries.reshape(length, HEADS, HEAD_DIM).astype(jnp.float32)
    key_f = keys.reshape(length, HEADS, HEAD_DIM).astype(jnp.float32)
    value_f = values.reshape(length, HEADS, HEAD_DIM).astype(jnp.float32)
    grad_f = cot_rec.reshape(length, HEADS, HEAD_DIM).astype(jnp.float32)
    scores = jnp.einsum('qhe,khe->hqk', query_f, key_f) * scale
    top = lax.optimization_barrier(jnp.max(scores, -1, keepdims=True))
    lse = top + jnp.log(lax.optimization_barrier(jnp.sum(jnp.exp(scores - top), -1, keepdims=True)))
    probs = jnp.exp(scores - lse)
    outputs = jnp.einsum('hqk,khe->qhe', probs, value_f, precision=lax.Precision.HIGHEST)
    delta = jnp.transpose(lax.optimization_barrier(jnp.sum(grad_f * outputs, -1)))[:, :, None]
    value_grad = jnp.einsum('hqk,qhe->khe', lowered(probs), grad_f).astype(jnp.bfloat16)
    prob_grad = jnp.einsum('qhe,khe->hqk', grad_f, value_f)
    score_half = lowered(probs * (prob_grad - delta))
    query_grad = (jnp.einsum('hqk,khe->qhe', score_half, key_f) * scale).astype(jnp.bfloat16)
    key_grad = (jnp.einsum('hqk,qhe->khe', score_half, query_f) * scale).astype(jnp.bfloat16)
    hidden_grad = jnp.dot(query_grad.reshape(length, HD), query_weight.T, preferred_element_type=jnp.float32)
    hidden_grad = hidden_grad + jnp.dot(key_grad.reshape(length, HD), key_weight.T, preferred_element_type=jnp.float32)
    hidden_grad = hidden_grad + jnp.dot(value_grad.reshape(length, HD), value_weight.T, preferred_element_type=jnp.float32)
    hidden_grad = hidden_grad.astype(jnp.bfloat16)
    normed_grad = jnp.dot(hidden_grad, proj_weight.T, preferred_element_type=jnp.float32)
    act_grad = inv_std * (normed_grad - lax.optimization_barrier(jnp.mean(normed_grad, -1, keepdims=True)) - normed * lax.optimization_barrier(jnp.mean(normed_grad * normed, -1, keepdims=True)))
    conv_grad = (act_grad * gelu_slope(conv_out)).astype(jnp.bfloat16)
    kernel_terms = jnp.concatenate([jnp.dot(taps[offset].T, conv_grad, preferred_element_type=jnp.float32) for offset in range(3)], 0)
    first = jnp.dot(conv_grad, conv_weight[0].T, preferred_element_type=jnp.float32)
    second = jnp.dot(conv_grad, conv_weight[1].T, preferred_element_type=jnp.float32)
    third = jnp.dot(conv_grad, conv_weight[2].T, preferred_element_type=jnp.float32)
    moved = jnp.concatenate([jnp.zeros((1, C), jnp.float32), third[:-1]], 0)
    even_rows = first + moved
    frame_rows = jnp.stack([even_rows, second], 1).reshape(2 * length, C).astype(jnp.bfloat16)
    return (kernel_terms, frame_rows)

def reference(frames, conv_weight, proj_weight, query_weight, key_weight, value_weight, cotangent):

    def per_record(record_pair):
        return one_record(record_pair[0], record_pair[1], conv_weight, proj_weight, query_weight, key_weight, value_weight)
    kernel_all, frame_grad = lax.map(per_record, (frames, cotangent))
    return (lax.optimization_barrier(jnp.sum(kernel_all, 0)), frame_grad)
```

```python
import functools
import math

import jax
import jax.numpy as jnp
from jax import lax
from jax.experimental import pallas as pl
from jax.experimental.pallas import tpu as pltpu
from jax.sharding import PartitionSpec as P

HEADS = 6
HEAD_DIM = 64


SQRT_HALF = 0.7071067811865476
INV_ROOT_TAU = 0.3989422804014327
EPSILON = 1e-05


def from_behind(value, axis, steps):
    count = lax.axis_size(axis)
    initial, last = (max(0, -steps), min(count, count - steps))
    return lax.ppermute(value, axis, [(source, source + steps) for source in range(initial, last)])


def gelu_slope(pre):
    return 0.5 * (1.0 + lax.erf(pre * SQRT_HALF)) + pre * INV_ROOT_TAU * jnp.exp(-0.5 * pre * pre)


def blocked(step_fn, carry, piece):
    rows = piece[0].shape[0]
    block_rows = math.gcd(rows, 512)
    block_count = rows // block_rows
    stacked = tuple(
        (member.reshape((block_count, block_rows) + member.shape[1:]) for member in piece)
    )

    def inner(state, item):
        block_index, members = item
        return (step_fn(state, members, block_index * block_rows), None)

    final, unused = lax.scan(inner, carry, (jnp.arange(block_count, dtype=jnp.int32), stacked))
    return final


def local(frames, conv_weight, proj_weight, query_weight, key_weight, value_weight, cotangent):
    inputs = frames[0]
    count = inputs.shape[0] // 2
    width = inputs.shape[1]
    following = from_behind(inputs[:1], "ctx", -1)
    paired = inputs.reshape(count, 2, width)
    tap_first = paired[:, 0]
    tap_second = paired[:, 1]
    tap_third = jnp.concatenate([tap_first[1:], following], 0)
    conv_out = jnp.dot(tap_first, conv_weight[0], preferred_element_type=jnp.float32)
    conv_out = conv_out + jnp.dot(tap_second, conv_weight[1], preferred_element_type=jnp.float32)
    conv_out = conv_out + jnp.dot(tap_third, conv_weight[2], preferred_element_type=jnp.float32)
    activated = jax.nn.gelu(conv_out, approximate=False)
    centre = jnp.mean(activated, -1, keepdims=True)
    spread = jnp.mean((activated - centre) ** 2, -1, keepdims=True)
    inv_std = lax.rsqrt(spread + EPSILON)
    normed = (activated - centre) * inv_std
    hidden = jnp.dot(
        normed.astype(jnp.bfloat16), proj_weight, preferred_element_type=jnp.float32
    ).astype(jnp.bfloat16)
    queries = jnp.dot(hidden, query_weight, preferred_element_type=jnp.float32).astype(jnp.bfloat16)
    keys = jnp.dot(hidden, key_weight, preferred_element_type=jnp.float32).astype(jnp.bfloat16)
    values = jnp.dot(hidden, value_weight, preferred_element_type=jnp.float32).astype(jnp.bfloat16)
    upstream = cotangent[0]
    scale = HEAD_DIM ** (-0.5)
    query_heads = queries.reshape(count, HEADS, HEAD_DIM)
    key_heads = keys.reshape(count, HEADS, HEAD_DIM)
    value_heads = values.reshape(count, HEADS, HEAD_DIM)
    grad_heads = upstream.reshape(count, HEADS, HEAD_DIM)

    def forward_block(carry, piece, start):
        running_top, running_total, accum = carry
        rows = piece[0].shape[0]
        keys_part = piece[0].reshape(rows, HEADS, HEAD_DIM)
        values_part = piece[1].reshape(rows, HEADS, HEAD_DIM)
        scores = (
            jnp.einsum("qhe,khe->hqk", query_heads, keys_part, preferred_element_type=jnp.float32)
            * scale
        )
        new_top = jnp.maximum(running_top, jnp.max(scores, -1))
        factor = jnp.exp(running_top - new_top)
        weights = jnp.exp(scores - new_top[:, :, None])
        new_total = running_total * factor + jnp.sum(weights, -1)
        new_accum = accum * jnp.transpose(factor)[:, :, None] + jnp.einsum(
            "hqk,khe->qhe",
            weights,
            values_part.astype(jnp.float32),
            precision=lax.Precision.HIGHEST,
        )
        return (new_top, new_total, new_accum)

    start_state = (
        jnp.full((HEADS, count), -jnp.inf, jnp.float32),
        jnp.zeros((HEADS, count), jnp.float32),
        jnp.zeros((count, HEADS, HEAD_DIM), jnp.float32),
    )
    final_top, final_total, final_accum = blocked(
        forward_block,
        start_state,
        (
            lax.all_gather(keys, "ctx", axis=0, tiled=True),
            lax.all_gather(values, "ctx", axis=0, tiled=True),
        ),
    )
    lse_heads = final_top + jnp.log(final_total)
    outputs = final_accum / jnp.transpose(final_total)[:, :, None]
    delta_rows = jnp.sum(grad_heads.astype(jnp.float32) * outputs, -1)
    delta_heads = jnp.transpose(delta_rows)

    def query_block(carry, piece, start):
        rows = piece[0].shape[0]
        keys_part = piece[0].reshape(rows, HEADS, HEAD_DIM)
        values_part = piece[1].reshape(rows, HEADS, HEAD_DIM)
        scores = (
            jnp.einsum("qhe,khe->hqk", query_heads, keys_part, preferred_element_type=jnp.float32)
            * scale
        )
        probs = jnp.exp(scores - lse_heads[:, :, None])
        prob_grad = jnp.einsum(
            "qhe,khe->hqk", grad_heads, values_part, preferred_element_type=jnp.float32
        )
        score_grad = probs * (prob_grad - delta_heads[:, :, None])
        return carry + jnp.einsum(
            "hqk,khe->qhe",
            score_grad.astype(jnp.bfloat16),
            keys_part,
            preferred_element_type=jnp.float32,
        )

    query_start = jnp.zeros((count, HEADS, HEAD_DIM), jnp.float32)
    query_accum = blocked(
        query_block,
        query_start,
        (
            lax.all_gather(keys, "ctx", axis=0, tiled=True),
            lax.all_gather(values, "ctx", axis=0, tiled=True),
        ),
    )
    query_grad = (query_accum * scale).astype(jnp.bfloat16).reshape(count, HEADS * HEAD_DIM)
    all_lse, all_delta = (
        lax.all_gather(jnp.transpose(lse_heads), "ctx", axis=0, tiled=True),
        lax.all_gather(delta_rows, "ctx", axis=0, tiled=True),
    )

    def key_block(carry, piece, start):
        key_accum, value_accum = carry
        rows = piece[0].shape[0]
        query_part = piece[0].reshape(rows, HEADS, HEAD_DIM)
        grad_part = piece[1].reshape(rows, HEADS, HEAD_DIM)
        lse_part = jnp.transpose(lax.dynamic_slice_in_dim(all_lse, start, rows, 0))
        delta_part = jnp.transpose(lax.dynamic_slice_in_dim(all_delta, start, rows, 0))
        scores = (
            jnp.einsum("qhe,khe->hqk", query_part, key_heads, preferred_element_type=jnp.float32)
            * scale
        )
        probs = jnp.exp(scores - lse_part[:, :, None])
        value_accum = value_accum + jnp.einsum(
            "hqk,qhe->khe",
            probs.astype(jnp.bfloat16),
            grad_part,
            preferred_element_type=jnp.float32,
        )
        prob_grad = jnp.einsum(
            "qhe,khe->hqk", grad_part, value_heads, preferred_element_type=jnp.float32
        )
        score_grad = probs * (prob_grad - delta_part[:, :, None])
        key_accum = key_accum + jnp.einsum(
            "hqk,qhe->khe",
            score_grad.astype(jnp.bfloat16),
            query_part,
            preferred_element_type=jnp.float32,
        )
        return (key_accum, value_accum)

    key_start = (
        jnp.zeros((count, HEADS, HEAD_DIM), jnp.float32),
        jnp.zeros((count, HEADS, HEAD_DIM), jnp.float32),
    )
    key_accum, value_accum = blocked(
        key_block,
        key_start,
        (
            lax.all_gather(queries, "ctx", axis=0, tiled=True),
            lax.all_gather(upstream, "ctx", axis=0, tiled=True),
        ),
    )
    key_grad = (key_accum * scale).astype(jnp.bfloat16).reshape(count, HEADS * HEAD_DIM)
    value_grad = value_accum.astype(jnp.bfloat16).reshape(count, HEADS * HEAD_DIM)
    hidden_grad = jnp.einsum(
        "tk,dk->td", query_grad, query_weight, preferred_element_type=jnp.float32
    )
    hidden_grad = hidden_grad + jnp.einsum(
        "tk,dk->td", key_grad, key_weight, preferred_element_type=jnp.float32
    )
    hidden_grad = hidden_grad + jnp.einsum(
        "tk,dk->td", value_grad, value_weight, preferred_element_type=jnp.float32
    )
    hidden_grad = hidden_grad.astype(jnp.bfloat16)
    normed_grad = jnp.einsum(
        "td,cd->tc", hidden_grad, proj_weight, preferred_element_type=jnp.float32
    )
    act_grad = inv_std * (
        normed_grad
        - jnp.mean(normed_grad, -1, keepdims=True)
        - normed * jnp.mean(normed_grad * normed, -1, keepdims=True)
    )
    conv_grad = (act_grad * gelu_slope(conv_out)).astype(jnp.bfloat16)
    kernel_terms = jnp.concatenate(
        [
            jnp.einsum("tc,to->co", tap_first, conv_grad, preferred_element_type=jnp.float32),
            jnp.einsum("tc,to->co", tap_second, conv_grad, preferred_element_type=jnp.float32),
            jnp.einsum("tc,to->co", tap_third, conv_grad, preferred_element_type=jnp.float32),
        ],
        0,
    )
    earlier = from_behind(conv_grad[count - 1 :], "ctx", 1)
    first = jnp.einsum("to,co->tc", conv_grad, conv_weight[0], preferred_element_type=jnp.float32)
    second = jnp.einsum("to,co->tc", conv_grad, conv_weight[1], preferred_element_type=jnp.float32)
    third = jnp.einsum("to,co->tc", conv_grad, conv_weight[2], preferred_element_type=jnp.float32)
    incoming = jnp.einsum("to,co->tc", earlier, conv_weight[2], preferred_element_type=jnp.float32)
    moved = jnp.concatenate([incoming, third[:-1]], 0)
    even_rows = first + moved
    frame_rows = jnp.stack([even_rows, second], 1).reshape(2 * count, width).astype(jnp.bfloat16)
    frame_sum = lax.psum_scatter(
        kernel_terms.astype(jnp.bfloat16), "ctx", scatter_dimension=0, tiled=True
    )
    weight_grad = lax.psum_scatter(frame_sum, "dp", scatter_dimension=1, tiled=True).astype(
        jnp.float32
    )
    return (weight_grad, frame_rows[None])


MESH = pl.DeviceIdType.MESH
ROW_ROW = (((1,), (1,)), ((), ()))
COL_COL = (((0,), (0,)), ((), ()))
PAIR = 2 * HEAD_DIM


def product(left, right, dims=(((1,), (0,)), ((), ()))):
    return lax.dot_general(left, right, dims, preferred_element_type=jnp.float32)


def normalised(conv_out):
    activated = 0.5 * conv_out * (1.0 + lax.erf(conv_out * SQRT_HALF))
    centre = jnp.mean(activated, -1, keepdims=True)
    spread = jnp.mean((activated - centre) ** 2, -1, keepdims=True)
    inv_std = lax.rsqrt(spread + EPSILON)
    return (activated - centre) * inv_std, inv_std


def fused(
    dp_size, ctx_size, count,
    frames, upstream, conv_hbm, proj_hbm, query_hbm, key_hbm, value_hbm,
    weight_out, frame_out,
    taps, cots, conv_w, proj_w, query_w, key_w, value_w,
    conv_all, q_all, k_all, v_all, stats, grads, cgs, window, z_send, z_recv,
    load_sem, frame_send, frame_recv, cot_send, cot_recv, stat_send, stat_recv,
    cg_send, cg_recv, zs_sem, zr_sem,
):
    me = lax.axis_index("ctx")
    record = lax.axis_index("dp")
    chips = ctx_size // 2
    chip, core = me // 2, me % 2
    sibling = chip * 2 + (1 - core)
    width = frames.shape[1]
    chan = width // 2
    total = ctx_size * count
    own = pl.ds(pl.multiple_of(me * count, count), count)

    def rows_of(index):
        return pl.ds(pl.multiple_of(index * count, count), count)

    def peer(step):
        return lax.rem(chip + step, chips) * 2 + core

    loads = []
    for slot, (source, target) in enumerate(
        [
            (frames, taps.at[own, pl.ds(0, width)]),
            (conv_hbm, conv_w),
            (proj_hbm, proj_w),
            (query_hbm, query_w),
            (key_hbm, key_w),
            (value_hbm, value_w),
            (upstream, cots.at[own]),
        ]
    ):
        load = pltpu.make_async_copy(source, target, load_sem.at[slot])
        load.start()
        loads.append(load)

    barrier = pltpu.get_barrier_semaphore()
    for step in range(1, ctx_size):
        pl.semaphore_signal(
            barrier, inc=1, device_id=(record, lax.rem(me + step, ctx_size)), device_id_type=MESH
        )
    for step in range(1, dp_size):
        pl.semaphore_signal(
            barrier, inc=1, device_id=(lax.rem(record + step, dp_size), me), device_id_type=MESH
        )
    pl.semaphore_wait(barrier, ctx_size - 1 + dp_size - 1)

    def transfer(view, send, recv, index, target, slot):
        return pltpu.make_async_remote_copy(
            src_ref=view(index),
            dst_ref=view(index),
            send_sem=send.at[slot],
            recv_sem=recv.at[index],
            device_id=(record, target),
            device_id_type=MESH,
        )

    def scatter(view, send, recv):
        copies = []
        for step in range(1, chips):
            copies.append(transfer(view, send, recv, me, peer(step), step))
        copies.append(transfer(view, send, recv, me, sibling, 0))
        for copy in copies:
            copy.start()
        return copies

    def collect(view, send, recv, copies):
        for step in range(1, chips):
            source = peer(chips - step)
            copy = transfer(view, send, recv, source, sibling, chips - 1 + step)
            copy.wait_recv()
            copy.start()
            copies.append(copy)
        for step in range(chips):
            source = lax.rem(chip + chips - step, chips) * 2 + (1 - core)
            transfer(view, send, recv, source, sibling, 0).wait_recv()

    def finish(copies):
        for copy in copies:
            copy.wait_send()

    def frame_view(index):
        return taps.at[rows_of(index), pl.ds(0, width)]

    def cot_view(index):
        return cots.at[rows_of(index)]

    def cg_view(index):
        return cgs.at[rows_of(index)]

    loads[0].wait()
    frame_copies = scatter(frame_view, frame_send, frame_recv)
    loads[6].wait()
    cot_copies = scatter(cot_view, cot_send, cot_recv)
    collect(frame_view, frame_send, frame_recv, frame_copies)

    part = math.gcd(total, 256)
    last_row = lax.broadcasted_iota(jnp.int32, (total, chan), 0) == total - 1
    even = taps[:, 0:chan].astype(jnp.float32)
    taps[:, width : width + chan] = jnp.where(
        last_row, 0.0, pltpu.roll(even, total - 1, 0)
    ).astype(jnp.bfloat16)
    for load in loads[1:6]:
        load.wait()
    for start in range(0, total, part):
        span = slice(start, start + part)
        conv_out = product(taps[span, :], conv_w[...])
        conv_all[span, :] = conv_out
        normed = normalised(conv_out)[0]
        hidden = product(normed.astype(jnp.bfloat16), proj_w[...]).astype(jnp.bfloat16)
        q_all[span, :] = product(hidden, query_w[...]).astype(jnp.bfloat16)
        k_all[span, :] = product(hidden, key_w[...]).astype(jnp.bfloat16)
        v_all[span, :] = product(hidden, value_w[...]).astype(jnp.bfloat16)

    scale = HEAD_DIM ** (-0.5)
    lanes = lax.broadcasted_iota(jnp.int32, (count, PAIR), 1)
    low = (lanes < HEAD_DIM).astype(jnp.float32).astype(jnp.bfloat16)
    high = (lanes >= HEAD_DIM).astype(jnp.float32).astype(jnp.bfloat16)

    def spread_pair(block):
        return jnp.concatenate([block * low, block * high], 0)

    def join_pair(square):
        return jnp.where(lanes < HEAD_DIM, square[:count], square[count:])

    pairs = HEADS // 2
    features = HEADS * HEAD_DIM
    stats[me] = jnp.zeros(stats.shape[1:], jnp.float32)
    saved = []
    for pair in range(pairs):
        cols = slice(pair * PAIR, (pair + 1) * PAIR)
        scores = product(k_all[:, cols], spread_pair(q_all[own, cols]), ROW_ROW) * scale
        prob_grad = product(v_all[:, cols], spread_pair(cots[own, cols]), ROW_ROW)
        top = jnp.max(scores, 0, keepdims=True)
        weights = jnp.exp(scores - top)
        mass = jnp.sum(weights, 0, keepdims=True)
        probs = weights / mass
        delta = jnp.sum(probs * prob_grad, 0, keepdims=True)
        stats[me, pair : pair + 1, :] = top + jnp.log(mass)
        stats[me, 4 + pair : 5 + pair, :] = delta
        saved.append((probs * (prob_grad - delta)).astype(jnp.bfloat16))
    stat_copies = []
    for step in range(1, ctx_size):
        copy = pltpu.make_async_remote_copy(
            src_ref=stats.at[me],
            dst_ref=stats.at[me],
            send_sem=stat_send.at[step],
            recv_sem=stat_recv.at[me],
            device_id=(record, lax.rem(me + step, ctx_size)),
            device_id_type=MESH,
        )
        copy.start()
        stat_copies.append(copy)
    for pair in range(pairs):
        cols = slice(pair * PAIR, (pair + 1) * PAIR)
        square = product(saved[pair], k_all[:, cols], COL_COL)
        grads[:, cols] = (join_pair(square) * scale).astype(jnp.bfloat16)
    collect(cot_view, cot_send, cot_recv, cot_copies)
    first_products = []
    for pair in range(pairs):
        cols = slice(pair * PAIR, (pair + 1) * PAIR)
        first_products.append(
            (
                product(spread_pair(k_all[own, cols]), q_all[:, cols], ROW_ROW) * scale,
                product(spread_pair(v_all[own, cols]), cots[:, cols], ROW_ROW),
            )
        )
    for step in range(1, ctx_size):
        source = lax.rem(me + step, ctx_size)
        pltpu.make_async_remote_copy(
            src_ref=stats.at[source],
            dst_ref=stats.at[source],
            send_sem=stat_send.at[step],
            recv_sem=stat_recv.at[source],
            device_id=(record, source),
            device_id_type=MESH,
        ).wait_recv()

    def along(row):
        halves = []
        for start in (0, HEAD_DIM):
            line = jnp.concatenate(
                [stats[index, row : row + 1, start : start + count] for index in range(ctx_size)], 1
            )
            halves.append(jnp.broadcast_to(line, (count, total)))
        return jnp.concatenate(halves, 0)

    for pair in range(pairs):
        cols = slice(pair * PAIR, (pair + 1) * PAIR)
        scores, prob_grad = first_products[pair]
        probs = jnp.exp(scores - along(pair))
        value_square = product(probs.astype(jnp.bfloat16), cots[:, cols])
        score_grad = (probs * (prob_grad - along(4 + pair))).astype(jnp.bfloat16)
        key_square = product(score_grad, q_all[:, cols])
        at_key = features + pair * PAIR
        at_value = 2 * features + pair * PAIR
        grads[:, at_key : at_key + PAIR] = (join_pair(key_square) * scale).astype(jnp.bfloat16)
        grads[:, at_value : at_value + PAIR] = join_pair(value_square).astype(jnp.bfloat16)

    hidden_grad = product(grads[:, 0:features], query_w[...], ROW_ROW)
    hidden_grad += product(grads[:, features : 2 * features], key_w[...], ROW_ROW)
    hidden_grad += product(grads[:, 2 * features : 3 * features], value_w[...], ROW_ROW)
    normed_grad = product(hidden_grad.astype(jnp.bfloat16), proj_w[...], ROW_ROW)
    conv_out = conv_all[own, :]
    normed, inv_std = normalised(conv_out)
    act_grad = inv_std * (
        normed_grad
        - jnp.mean(normed_grad, -1, keepdims=True)
        - normed * jnp.mean(normed_grad * normed, -1, keepdims=True)
    )
    conv_grad = (act_grad * gelu_slope(conv_out)).astype(jnp.bfloat16)
    cgs[own, :] = conv_grad
    cg_copies = scatter(cg_view, cg_send, cg_recv)
    frame_out[:, chan:width] = product(
        conv_grad, conv_w[chan : 2 * chan, :], ROW_ROW
    ).astype(jnp.bfloat16)
    even_rows = product(conv_grad, conv_w[0:chan, :], ROW_ROW)
    collect(cg_view, cg_send, cg_recv, cg_copies)

    share = weight_out.shape[0]
    columns = weight_out.shape[1]
    base = (me * share) // 128 * 128
    picked = taps[:, pl.ds(pl.multiple_of(base, 128), 256)]
    window[...] = product(picked, cgs[...], COL_COL)
    shift = me * share - base
    terms = window[pl.ds(pl.multiple_of(shift, 64), share), :]
    for index in range(dp_size):
        z_send[index] = terms[:, index * columns : (index + 1) * columns].astype(jnp.bfloat16)
    z_copies = []
    for step in range(1, dp_size):
        target = lax.rem(record + step, dp_size)
        copy = pltpu.make_async_remote_copy(
            src_ref=z_send.at[target],
            dst_ref=z_recv.at[record],
            send_sem=zs_sem.at[step],
            recv_sem=zr_sem.at[record],
            device_id=(target, me),
            device_id_type=MESH,
        )
        copy.start()
        z_copies.append(copy)
    before = lax.rem(me + ctx_size - 1, ctx_size)
    tail = cgs[pl.ds(pl.multiple_of(before * count + count - 16, 16), 16), :].astype(jnp.float32)
    incoming = jnp.where(me > 0, tail[15:16, :], 0.0)
    first_row = lax.broadcasted_iota(jnp.int32, (count, chan), 0) == 0
    moved = pltpu.roll(cgs[own, :].astype(jnp.float32), 1, 0)
    moved = jnp.where(first_row, incoming, moved).astype(jnp.bfloat16)
    even_rows = even_rows + product(moved, conv_w[2 * chan : 3 * chan, :], ROW_ROW)
    frame_out[:, 0:chan] = even_rows.astype(jnp.bfloat16)

    result = z_send[record].astype(jnp.float32)
    for step in range(1, dp_size):
        source = lax.rem(record + step, dp_size)
        pltpu.make_async_remote_copy(
            src_ref=z_recv.at[source],
            dst_ref=z_recv.at[source],
            send_sem=zs_sem.at[step],
            recv_sem=zr_sem.at[source],
            device_id=(source, me),
            device_id_type=MESH,
        ).wait_recv()
        result = result + z_recv[source].astype(jnp.float32)
    weight_out[...] = result
    for copies in (frame_copies, cot_copies, stat_copies, cg_copies, z_copies):
        finish(copies)


def local_fused(
    dp_size, ctx_size,
    frames, conv_weight, proj_weight, query_weight, key_weight, value_weight, cotangent,
):
    inputs = frames[0]
    count, chan = inputs.shape[0] // 2, inputs.shape[1]
    total = ctx_size * count
    depth, features = query_weight.shape
    share, columns = 3 * chan // ctx_size, chan // dp_size
    half = jnp.bfloat16
    dma = pltpu.SemaphoreType.DMA
    weight_grad, frame_rows = pl.pallas_call(
        functools.partial(fused, dp_size, ctx_size, count),
        out_shape=(
            jax.ShapeDtypeStruct((share, columns), jnp.float32),
            jax.ShapeDtypeStruct((count, 2 * chan), half),
        ),
        in_specs=[pl.BlockSpec(memory_space=pl.ANY)] * 7,
        out_specs=[pl.BlockSpec(memory_space=pltpu.VMEM)] * 2,
        scratch_shapes=[
            pltpu.VMEM((total, 3 * chan), half),
            pltpu.VMEM((total, features), half),
            pltpu.VMEM((3 * chan, chan), half),
            pltpu.VMEM((chan, depth), half),
            pltpu.VMEM((depth, features), half),
            pltpu.VMEM((depth, features), half),
            pltpu.VMEM((depth, features), half),
            pltpu.VMEM((total, chan), jnp.float32),
            pltpu.VMEM((total, features), half),
            pltpu.VMEM((total, features), half),
            pltpu.VMEM((total, features), half),
            pltpu.VMEM((ctx_size, 8, PAIR), jnp.float32),
            pltpu.VMEM((count, 3 * features), half),
            pltpu.VMEM((total, chan), half),
            pltpu.VMEM((256, chan), jnp.float32),
            pltpu.VMEM((dp_size, share, columns), half),
            pltpu.VMEM((dp_size, share, columns), half),
            dma((7,)),
            dma((ctx_size,)),
            dma((ctx_size,)),
            dma((ctx_size,)),
            dma((ctx_size,)),
            dma((ctx_size,)),
            dma((ctx_size,)),
            dma((ctx_size,)),
            dma((ctx_size,)),
            dma((dp_size,)),
            dma((dp_size,)),
        ],
        compiler_params=pltpu.CompilerParams(
            collective_id=0, has_side_effects=True, vmem_limit_bytes=48 * 2**20
        ),
    )(
        inputs.reshape(count, 2 * chan),
        cotangent[0],
        conv_weight.reshape(3 * chan, chan),
        proj_weight,
        query_weight,
        key_weight,
        value_weight,
    )
    return weight_grad, frame_rows.reshape(1, 2 * count, chan)


def solution(mesh):
    in_specs = (P("dp", "ctx", None), P(), P(), P(), P(), P(), P("dp", "ctx", None))
    out_specs = (P("ctx", "dp"), P("dp", "ctx", None))
    dp_size, ctx_size = mesh.shape["dp"], mesh.shape["ctx"]

    def plan(frames, *others):
        count, chan = frames.shape[1] // 2, frames.shape[2]
        share = 3 * chan // ctx_size
        fits = count == HEAD_DIM and ctx_size % 2 == 0 and ctx_size * count <= 512
        if fits and chan % (128 * dp_size) == 0 and share == 192:
            return local_fused(dp_size, ctx_size, frames, *others)
        return local(frames, *others)

    return jax.shard_map(plan, mesh=mesh, in_specs=in_specs, out_specs=out_specs, check_vma=False)
```

```python
import functools
import math

import jax
import jax.numpy as jnp
from jax import lax
from jax.experimental import pallas as pl
from jax.experimental.pallas import tpu as pltpu
from jax.sharding import PartitionSpec as P

HEADS = 6
HEAD_DIM = 64


SQRT_HALF = 0.7071067811865476
INV_ROOT_TAU = 0.3989422804014327
EPSILON = 1e-05


def from_behind(value, axis, steps):
    count = lax.axis_size(axis)
    initial, last = (max(0, -steps), min(count, count - steps))
    return lax.ppermute(value, axis, [(source, source + steps) for source in range(initial, last)])


def gelu_slope(pre):
    return 0.5 * (1.0 + lax.erf(pre * SQRT_HALF)) + pre * INV_ROOT_TAU * jnp.exp(-0.5 * pre * pre)


def blocked(step_fn, carry, piece):
    rows = piece[0].shape[0]
    block_rows = math.gcd(rows, 512)
    block_count = rows // block_rows
    stacked = tuple(
        (member.reshape((block_count, block_rows) + member.shape[1:]) for member in piece)
    )

    def inner(state, item):
        block_index, members = item
        return (step_fn(state, members, block_index * block_rows), None)

    final, unused = lax.scan(inner, carry, (jnp.arange(block_count, dtype=jnp.int32), stacked))
    return final


def local(frames, conv_weight, proj_weight, query_weight, key_weight, value_weight, cotangent):
    inputs = frames[0]
    count = inputs.shape[0] // 2
    width = inputs.shape[1]
    following = from_behind(inputs[:1], "ctx", -1)
    paired = inputs.reshape(count, 2, width)
    tap_first = paired[:, 0]
    tap_second = paired[:, 1]
    tap_third = jnp.concatenate([tap_first[1:], following], 0)
    conv_out = jnp.dot(tap_first, conv_weight[0], preferred_element_type=jnp.float32)
    conv_out = conv_out + jnp.dot(tap_second, conv_weight[1], preferred_element_type=jnp.float32)
    conv_out = conv_out + jnp.dot(tap_third, conv_weight[2], preferred_element_type=jnp.float32)
    activated = jax.nn.gelu(conv_out, approximate=False)
    centre = jnp.mean(activated, -1, keepdims=True)
    spread = jnp.mean((activated - centre) ** 2, -1, keepdims=True)
    inv_std = lax.rsqrt(spread + EPSILON)
    normed = (activated - centre) * inv_std
    hidden = jnp.dot(
        normed.astype(jnp.bfloat16), proj_weight, preferred_element_type=jnp.float32
    ).astype(jnp.bfloat16)
    queries = jnp.dot(hidden, query_weight, preferred_element_type=jnp.float32).astype(jnp.bfloat16)
    keys = jnp.dot(hidden, key_weight, preferred_element_type=jnp.float32).astype(jnp.bfloat16)
    values = jnp.dot(hidden, value_weight, preferred_element_type=jnp.float32).astype(jnp.bfloat16)
    upstream = cotangent[0]
    scale = HEAD_DIM ** (-0.5)
    query_heads = queries.reshape(count, HEADS, HEAD_DIM)
    key_heads = keys.reshape(count, HEADS, HEAD_DIM)
    value_heads = values.reshape(count, HEADS, HEAD_DIM)
    grad_heads = upstream.reshape(count, HEADS, HEAD_DIM)

    def forward_block(carry, piece, start):
        running_top, running_total, accum = carry
        rows = piece[0].shape[0]
        keys_part = piece[0].reshape(rows, HEADS, HEAD_DIM)
        values_part = piece[1].reshape(rows, HEADS, HEAD_DIM)
        scores = (
            jnp.einsum("qhe,khe->hqk", query_heads, keys_part, preferred_element_type=jnp.float32)
            * scale
        )
        new_top = jnp.maximum(running_top, jnp.max(scores, -1))
        factor = jnp.exp(running_top - new_top)
        weights = jnp.exp(scores - new_top[:, :, None])
        new_total = running_total * factor + jnp.sum(weights, -1)
        new_accum = accum * jnp.transpose(factor)[:, :, None] + jnp.einsum(
            "hqk,khe->qhe",
            weights,
            values_part.astype(jnp.float32),
            precision=lax.Precision.HIGHEST,
        )
        return (new_top, new_total, new_accum)

    start_state = (
        jnp.full((HEADS, count), -jnp.inf, jnp.float32),
        jnp.zeros((HEADS, count), jnp.float32),
        jnp.zeros((count, HEADS, HEAD_DIM), jnp.float32),
    )
    final_top, final_total, final_accum = blocked(
        forward_block,
        start_state,
        (
            lax.all_gather(keys, "ctx", axis=0, tiled=True),
            lax.all_gather(values, "ctx", axis=0, tiled=True),
        ),
    )
    lse_heads = final_top + jnp.log(final_total)
    outputs = final_accum / jnp.transpose(final_total)[:, :, None]
    delta_rows = jnp.sum(grad_heads.astype(jnp.float32) * outputs, -1)
    delta_heads = jnp.transpose(delta_rows)

    def query_block(carry, piece, start):
        rows = piece[0].shape[0]
        keys_part = piece[0].reshape(rows, HEADS, HEAD_DIM)
        values_part = piece[1].reshape(rows, HEADS, HEAD_DIM)
        scores = (
            jnp.einsum("qhe,khe->hqk", query_heads, keys_part, preferred_element_type=jnp.float32)
            * scale
        )
        probs = jnp.exp(scores - lse_heads[:, :, None])
        prob_grad = jnp.einsum(
            "qhe,khe->hqk", grad_heads, values_part, preferred_element_type=jnp.float32
        )
        score_grad = probs * (prob_grad - delta_heads[:, :, None])
        return carry + jnp.einsum(
            "hqk,khe->qhe",
            score_grad.astype(jnp.bfloat16),
            keys_part,
            preferred_element_type=jnp.float32,
        )

    query_start = jnp.zeros((count, HEADS, HEAD_DIM), jnp.float32)
    query_accum = blocked(
        query_block,
        query_start,
        (
            lax.all_gather(keys, "ctx", axis=0, tiled=True),
            lax.all_gather(values, "ctx", axis=0, tiled=True),
        ),
    )
    query_grad = (query_accum * scale).astype(jnp.bfloat16).reshape(count, HEADS * HEAD_DIM)
    all_lse, all_delta = (
        lax.all_gather(jnp.transpose(lse_heads), "ctx", axis=0, tiled=True),
        lax.all_gather(delta_rows, "ctx", axis=0, tiled=True),
    )

    def key_block(carry, piece, start):
        key_accum, value_accum = carry
        rows = piece[0].shape[0]
        query_part = piece[0].reshape(rows, HEADS, HEAD_DIM)
        grad_part = piece[1].reshape(rows, HEADS, HEAD_DIM)
        lse_part = jnp.transpose(lax.dynamic_slice_in_dim(all_lse, start, rows, 0))
        delta_part = jnp.transpose(lax.dynamic_slice_in_dim(all_delta, start, rows, 0))
        scores = (
            jnp.einsum("qhe,khe->hqk", query_part, key_heads, preferred_element_type=jnp.float32)
            * scale
        )
        probs = jnp.exp(scores - lse_part[:, :, None])
        value_accum = value_accum + jnp.einsum(
            "hqk,qhe->khe",
            probs.astype(jnp.bfloat16),
            grad_part,
            preferred_element_type=jnp.float32,
        )
        prob_grad = jnp.einsum(
            "qhe,khe->hqk", grad_part, value_heads, preferred_element_type=jnp.float32
        )
        score_grad = probs * (prob_grad - delta_part[:, :, None])
        key_accum = key_accum + jnp.einsum(
            "hqk,qhe->khe",
            score_grad.astype(jnp.bfloat16),
            query_part,
            preferred_element_type=jnp.float32,
        )
        return (key_accum, value_accum)

    key_start = (
        jnp.zeros((count, HEADS, HEAD_DIM), jnp.float32),
        jnp.zeros((count, HEADS, HEAD_DIM), jnp.float32),
    )
    key_accum, value_accum = blocked(
        key_block,
        key_start,
        (
            lax.all_gather(queries, "ctx", axis=0, tiled=True),
            lax.all_gather(upstream, "ctx", axis=0, tiled=True),
        ),
    )
    key_grad = (key_accum * scale).astype(jnp.bfloat16).reshape(count, HEADS * HEAD_DIM)
    value_grad = value_accum.astype(jnp.bfloat16).reshape(count, HEADS * HEAD_DIM)
    hidden_grad = jnp.einsum(
        "tk,dk->td", query_grad, query_weight, preferred_element_type=jnp.float32
    )
    hidden_grad = hidden_grad + jnp.einsum(
        "tk,dk->td", key_grad, key_weight, preferred_element_type=jnp.float32
    )
    hidden_grad = hidden_grad + jnp.einsum(
        "tk,dk->td", value_grad, value_weight, preferred_element_type=jnp.float32
    )
    hidden_grad = hidden_grad.astype(jnp.bfloat16)
    normed_grad = jnp.einsum(
        "td,cd->tc", hidden_grad, proj_weight, preferred_element_type=jnp.float32
    )
    act_grad = inv_std * (
        normed_grad
        - jnp.mean(normed_grad, -1, keepdims=True)
        - normed * jnp.mean(normed_grad * normed, -1, keepdims=True)
    )
    conv_grad = (act_grad * gelu_slope(conv_out)).astype(jnp.bfloat16)
    kernel_terms = jnp.concatenate(
        [
            jnp.einsum("tc,to->co", tap_first, conv_grad, preferred_element_type=jnp.float32),
            jnp.einsum("tc,to->co", tap_second, conv_grad, preferred_element_type=jnp.float32),
            jnp.einsum("tc,to->co", tap_third, conv_grad, preferred_element_type=jnp.float32),
        ],
        0,
    )
    earlier = from_behind(conv_grad[count - 1 :], "ctx", 1)
    first = jnp.einsum("to,co->tc", conv_grad, conv_weight[0], preferred_element_type=jnp.float32)
    second = jnp.einsum("to,co->tc", conv_grad, conv_weight[1], preferred_element_type=jnp.float32)
    third = jnp.einsum("to,co->tc", conv_grad, conv_weight[2], preferred_element_type=jnp.float32)
    incoming = jnp.einsum("to,co->tc", earlier, conv_weight[2], preferred_element_type=jnp.float32)
    moved = jnp.concatenate([incoming, third[:-1]], 0)
    even_rows = first + moved
    frame_rows = jnp.stack([even_rows, second], 1).reshape(2 * count, width).astype(jnp.bfloat16)
    frame_sum = lax.psum_scatter(
        kernel_terms.astype(jnp.bfloat16), "ctx", scatter_dimension=0, tiled=True
    )
    weight_grad = lax.psum_scatter(frame_sum, "dp", scatter_dimension=1, tiled=True).astype(
        jnp.float32
    )
    return (weight_grad, frame_rows[None])


MESH = pl.DeviceIdType.MESH
ROW_ROW = (((1,), (1,)), ((), ()))
COL_COL = (((0,), (0,)), ((), ()))
PAIR = 2 * HEAD_DIM
GROUP = 2


def product(left, right, dims=(((1,), (0,)), ((), ()))):
    return lax.dot_general(left, right, dims, preferred_element_type=jnp.float32)


def normalised(conv_out):
    activated = 0.5 * conv_out * (1.0 + lax.erf(conv_out * SQRT_HALF))
    centre = jnp.mean(activated, -1, keepdims=True)
    spread = jnp.mean((activated - centre) ** 2, -1, keepdims=True)
    inv_std = lax.rsqrt(spread + EPSILON)
    return (activated - centre) * inv_std, inv_std


def fused(
    dp_size, ctx_size, count,
    frames, upstream, conv_hbm, proj_hbm, query_hbm, key_hbm, value_hbm,
    weight_out, frame_out,
    taps, cots, conv_w, proj_w, query_w, key_w, value_w,
    conv_all, q_all, k_all, v_all, stats, grads, cgs, window, z_send, z_recv,
    load_sem, frame_send, frame_recv, cot_send, cot_recv, stat_send, stat_recv,
    cg_send, cg_recv, zs_sem, zr_sem,
):
    me = lax.axis_index("ctx")
    record = lax.axis_index("dp")
    chips = ctx_size // 2
    chip, core = me // 2, me % 2
    sibling = chip * 2 + (1 - core)
    width = frames.shape[1]
    chan = width // 2
    total = ctx_size * count
    own = pl.ds(pl.multiple_of(me * count, count), count)

    def rows_of(index):
        return pl.ds(pl.multiple_of(index * count, count), count)

    def peer(step):
        return lax.rem(chip + step, chips) * 2 + core

    loads = []
    for slot, (source, target) in enumerate(
        [
            (frames, taps.at[own, pl.ds(0, width)]),
            (conv_hbm, conv_w),
            (proj_hbm, proj_w),
            (query_hbm, query_w),
            (key_hbm, key_w),
            (value_hbm, value_w),
            (upstream, cots.at[own]),
        ]
    ):
        load = pltpu.make_async_copy(source, target, load_sem.at[slot])
        load.start()
        loads.append(load)

    barrier = pltpu.get_barrier_semaphore()
    for step in range(1, ctx_size):
        pl.semaphore_signal(
            barrier, inc=1, device_id=(record, lax.rem(me + step, ctx_size)), device_id_type=MESH
        )
    for step in range(1, dp_size):
        pl.semaphore_signal(
            barrier, inc=1, device_id=(lax.rem(record + step, dp_size), me), device_id_type=MESH
        )
    pl.semaphore_wait(barrier, ctx_size - 1 + dp_size - 1)

    def transfer(view, send, recv, index, target, slot):
        return pltpu.make_async_remote_copy(
            src_ref=view(index),
            dst_ref=view(index),
            send_sem=send.at[slot],
            recv_sem=recv.at[index],
            device_id=(record, target),
            device_id_type=MESH,
        )

    def scatter(view, send, recv):
        copies = []
        for step in range(1, chips):
            copies.append(transfer(view, send, recv, me, peer(chips - step), step))
        copies.append(transfer(view, send, recv, me, sibling, 0))
        for copy in copies:
            copy.start()
        return copies

    def pass_on(view, send, recv, copies, step):
        source = peer(step)
        copy = transfer(view, send, recv, source, sibling, chips - 1 + step)
        copy.wait_recv()
        copy.start()
        copies.append(copy)

    def arrive(view, send, recv, step):
        source = lax.rem(chip + step, chips) * 2 + (1 - core)
        transfer(view, send, recv, source, sibling, 0).wait_recv()

    def collect(view, send, recv, copies):
        for step in range(1, chips):
            pass_on(view, send, recv, copies, step)
        for step in range(chips):
            arrive(view, send, recv, step)

    def finish(copies):
        for copy in copies:
            copy.wait_send()

    def frame_view(index):
        return taps.at[rows_of(index), pl.ds(0, width)]

    def cot_view(index):
        return cots.at[rows_of(index)]

    def cg_view(half):
        return lambda index: cgs.at[rows_of(index), pl.ds(half * (chan // 2), chan // 2)]

    loads[0].wait()
    frame_copies = scatter(frame_view, frame_send, frame_recv)
    loads[6].wait()
    cot_copies = scatter(cot_view, cot_send, cot_recv)
    pair_rows = 2 * count
    last_row = lax.broadcasted_iota(jnp.int32, (pair_rows, chan), 0) == pair_rows - 1

    def pair_span(index):
        return pl.ds(pl.multiple_of(index * pair_rows, pair_rows), pair_rows)

    def forward(steps):
        spans = []
        for step in steps:
            here = lax.rem(chip + step, chips)
            after = lax.rem(here + 1, chips)
            span = pair_span(here)
            even = taps[span, 0:chan].astype(jnp.float32)
            head = taps[pl.ds(pl.multiple_of(after * pair_rows, 16), 16), 0:chan]
            following = jnp.where(here < chips - 1, head.astype(jnp.float32)[0:1, :], 0.0)
            taps[span, width : width + chan] = jnp.where(
                last_row, following, pltpu.roll(even, pair_rows - 1, 0)
            ).astype(jnp.bfloat16)
            spans.append(span)
        block = jnp.concatenate([taps[span, :] for span in spans], 0)
        conv_out = product(block, conv_w[...])
        normed = normalised(conv_out)[0]
        hidden = product(normed.astype(jnp.bfloat16), proj_w[...]).astype(jnp.bfloat16)
        queries = product(hidden, query_w[...]).astype(jnp.bfloat16)
        keys = product(hidden, key_w[...]).astype(jnp.bfloat16)
        values = product(hidden, value_w[...]).astype(jnp.bfloat16)
        for place, span in enumerate(spans):
            piece = slice(place * pair_rows, (place + 1) * pair_rows)
            conv_all[span, :] = conv_out[piece]
            q_all[span, :] = queries[piece]
            k_all[span, :] = keys[piece]
            v_all[span, :] = values[piece]

    for load in loads[1:6]:
        load.wait()
    arrive(frame_view, frame_send, frame_recv, 0)
    waiting = []
    for step in range(1, chips + 2):
        if step < chips:
            pass_on(frame_view, frame_send, frame_recv, frame_copies, step)
        if 1 < step <= chips:
            arrive(frame_view, frame_send, frame_recv, step - 1)
        if step > 1:
            waiting.append(step - 2)
        if len(waiting) == GROUP or (waiting and step == chips + 1):
            forward(waiting)
            waiting = []

    scale = HEAD_DIM ** (-0.5)
    lanes = lax.broadcasted_iota(jnp.int32, (count, PAIR), 1)
    low = (lanes < HEAD_DIM).astype(jnp.float32).astype(jnp.bfloat16)
    high = (lanes >= HEAD_DIM).astype(jnp.float32).astype(jnp.bfloat16)

    def spread_pair(block):
        return jnp.concatenate([block * low, block * high], 0)

    def join_pair(square):
        return jnp.where(lanes < HEAD_DIM, square[:count], square[count:])

    pairs = HEADS // 2
    features = HEADS * HEAD_DIM
    stats[me] = jnp.zeros(stats.shape[1:], jnp.float32)
    saved = []
    for pair in range(pairs):
        cols = slice(pair * PAIR, (pair + 1) * PAIR)
        scores = product(k_all[:, cols], spread_pair(q_all[own, cols]), ROW_ROW) * scale
        prob_grad = product(v_all[:, cols], spread_pair(cots[own, cols]), ROW_ROW)
        top = jnp.max(scores, 0, keepdims=True)
        weights = jnp.exp(scores - top)
        mass = jnp.sum(weights, 0, keepdims=True)
        probs = weights / mass
        delta = jnp.sum(probs * prob_grad, 0, keepdims=True)
        stats[me, pair : pair + 1, :] = top + jnp.log(mass)
        stats[me, 4 + pair : 5 + pair, :] = delta
        saved.append((probs * (prob_grad - delta)).astype(jnp.bfloat16))
    stat_copies = []
    for step in range(1, ctx_size):
        copy = pltpu.make_async_remote_copy(
            src_ref=stats.at[me],
            dst_ref=stats.at[me],
            send_sem=stat_send.at[step],
            recv_sem=stat_recv.at[me],
            device_id=(record, lax.rem(me + step, ctx_size)),
            device_id_type=MESH,
        )
        copy.start()
        stat_copies.append(copy)
    for pair in range(pairs):
        cols = slice(pair * PAIR, (pair + 1) * PAIR)
        square = product(saved[pair], k_all[:, cols], COL_COL)
        grads[:, cols] = (join_pair(square) * scale).astype(jnp.bfloat16)
    collect(cot_view, cot_send, cot_recv, cot_copies)
    first_products = []
    for pair in range(pairs):
        cols = slice(pair * PAIR, (pair + 1) * PAIR)
        first_products.append(
            (
                product(spread_pair(k_all[own, cols]), q_all[:, cols], ROW_ROW) * scale,
                product(spread_pair(v_all[own, cols]), cots[:, cols], ROW_ROW),
            )
        )
    for step in range(1, ctx_size):
        source = lax.rem(me + step, ctx_size)
        pltpu.make_async_remote_copy(
            src_ref=stats.at[source],
            dst_ref=stats.at[source],
            send_sem=stat_send.at[step],
            recv_sem=stat_recv.at[source],
            device_id=(record, source),
            device_id_type=MESH,
        ).wait_recv()

    def along(row):
        halves = []
        for start in (0, HEAD_DIM):
            line = jnp.concatenate(
                [stats[index, row : row + 1, start : start + count] for index in range(ctx_size)], 1
            )
            halves.append(jnp.broadcast_to(line, (count, total)))
        return jnp.concatenate(halves, 0)

    for pair in range(pairs):
        cols = slice(pair * PAIR, (pair + 1) * PAIR)
        scores, prob_grad = first_products[pair]
        probs = jnp.exp(scores - along(pair))
        value_square = product(probs.astype(jnp.bfloat16), cots[:, cols])
        score_grad = (probs * (prob_grad - along(4 + pair))).astype(jnp.bfloat16)
        key_square = product(score_grad, q_all[:, cols])
        at_key = features + pair * PAIR
        at_value = 2 * features + pair * PAIR
        grads[:, at_key : at_key + PAIR] = (join_pair(key_square) * scale).astype(jnp.bfloat16)
        grads[:, at_value : at_value + PAIR] = join_pair(value_square).astype(jnp.bfloat16)

    hidden_grad = product(grads[:, 0:features], query_w[...], ROW_ROW)
    hidden_grad += product(grads[:, features : 2 * features], key_w[...], ROW_ROW)
    hidden_grad += product(grads[:, 2 * features : 3 * features], value_w[...], ROW_ROW)
    normed_grad = product(hidden_grad.astype(jnp.bfloat16), proj_w[...], ROW_ROW)
    conv_out = conv_all[own, :]
    normed, inv_std = normalised(conv_out)
    act_grad = inv_std * (
        normed_grad
        - jnp.mean(normed_grad, -1, keepdims=True)
        - normed * jnp.mean(normed_grad * normed, -1, keepdims=True)
    )
    conv_grad = (act_grad * gelu_slope(conv_out)).astype(jnp.bfloat16)
    cgs[own, :] = conv_grad
    cg_parts = [
        scatter(cg_view(half), cg_send.at[half], cg_recv.at[half]) for half in range(2)
    ]
    frame_out[:, chan:width] = product(
        conv_grad, conv_w[chan : 2 * chan, :], ROW_ROW
    ).astype(jnp.bfloat16)
    even_rows = product(conv_grad, conv_w[0:chan, :], ROW_ROW)
    share = weight_out.shape[0]
    columns = weight_out.shape[1]
    base = (me * share) // 128 * 128
    shift = pl.multiple_of(me * share - base, 64)
    picked = taps[:, pl.ds(pl.multiple_of(base, 128), 256)]

    def z_copy(index):
        return pltpu.make_async_remote_copy(
            src_ref=z_send.at[index],
            dst_ref=z_recv.at[record],
            send_sem=zs_sem.at[index],
            recv_sem=zr_sem.at[record],
            device_id=(index, me),
            device_id_type=MESH,
        )

    for half in range(2):
        collect(cg_view(half), cg_send.at[half], cg_recv.at[half], cg_parts[half])
        side = slice(half * (chan // 2), (half + 1) * (chan // 2))
        window[:, side] = product(picked, cgs[:, side], COL_COL)
        for index in range(half * dp_size // 2, (half + 1) * dp_size // 2):
            z_send[index] = window[
                pl.ds(shift, share), index * columns : (index + 1) * columns
            ].astype(jnp.bfloat16)

            @pl.when(record != index)
            def _():
                z_copy(index).start()

    before = lax.rem(me + ctx_size - 1, ctx_size)
    tail = cgs[pl.ds(pl.multiple_of(before * count + count - 16, 16), 16), :].astype(jnp.float32)
    incoming = jnp.where(me > 0, tail[15:16, :], 0.0)
    first_row = lax.broadcasted_iota(jnp.int32, (count, chan), 0) == 0
    moved = pltpu.roll(cgs[own, :].astype(jnp.float32), 1, 0)
    moved = jnp.where(first_row, incoming, moved).astype(jnp.bfloat16)
    even_rows = even_rows + product(moved, conv_w[2 * chan : 3 * chan, :], ROW_ROW)
    frame_out[:, 0:chan] = even_rows.astype(jnp.bfloat16)

    result = z_send[record].astype(jnp.float32)
    for step in range(1, dp_size):
        source = lax.rem(record + step, dp_size)
        pltpu.make_async_remote_copy(
            src_ref=z_recv.at[source],
            dst_ref=z_recv.at[source],
            send_sem=zs_sem.at[source],
            recv_sem=zr_sem.at[source],
            device_id=(source, me),
            device_id_type=MESH,
        ).wait_recv()
        result = result + z_recv[source].astype(jnp.float32)
    weight_out[...] = result
    for copies in (frame_copies, cot_copies, stat_copies, cg_parts[0], cg_parts[1]):
        finish(copies)
    for index in range(dp_size):

        @pl.when(record != index)
        def _():
            z_copy(index).wait_send()


def local_fused(
    dp_size, ctx_size,
    frames, conv_weight, proj_weight, query_weight, key_weight, value_weight, cotangent,
):
    inputs = frames[0]
    count, chan = inputs.shape[0] // 2, inputs.shape[1]
    total = ctx_size * count
    depth, features = query_weight.shape
    share, columns = 3 * chan // ctx_size, chan // dp_size
    half = jnp.bfloat16
    dma = pltpu.SemaphoreType.DMA
    weight_grad, frame_rows = pl.pallas_call(
        functools.partial(fused, dp_size, ctx_size, count),
        out_shape=(
            jax.ShapeDtypeStruct((share, columns), jnp.float32),
            jax.ShapeDtypeStruct((count, 2 * chan), half),
        ),
        in_specs=[pl.BlockSpec(memory_space=pltpu.HBM)] * 7,
        out_specs=[pl.BlockSpec(memory_space=pltpu.VMEM)] * 2,
        scratch_shapes=[
            pltpu.VMEM((total, 3 * chan), half),
            pltpu.VMEM((total, features), half),
            pltpu.VMEM((3 * chan, chan), half),
            pltpu.VMEM((chan, depth), half),
            pltpu.VMEM((depth, features), half),
            pltpu.VMEM((depth, features), half),
            pltpu.VMEM((depth, features), half),
            pltpu.VMEM((total, chan), jnp.float32),
            pltpu.VMEM((total, features), half),
            pltpu.VMEM((total, features), half),
            pltpu.VMEM((total, features), half),
            pltpu.VMEM((ctx_size, 8, PAIR), jnp.float32),
            pltpu.VMEM((count, 3 * features), half),
            pltpu.VMEM((total, chan), half),
            pltpu.VMEM((256, chan), jnp.float32),
            pltpu.VMEM((dp_size, share, columns), half),
            pltpu.VMEM((dp_size, share, columns), half),
            dma((7,)),
            dma((ctx_size,)),
            dma((ctx_size,)),
            dma((ctx_size,)),
            dma((ctx_size,)),
            dma((ctx_size,)),
            dma((ctx_size,)),
            dma((2, ctx_size)),
            dma((2, ctx_size)),
            dma((dp_size,)),
            dma((dp_size,)),
        ],
        compiler_params=pltpu.CompilerParams(
            collective_id=0, has_side_effects=True, vmem_limit_bytes=60 * 2**20
        ),
    )(
        inputs.reshape(count, 2 * chan),
        cotangent[0],
        conv_weight.reshape(3 * chan, chan),
        proj_weight,
        query_weight,
        key_weight,
        value_weight,
    )
    return weight_grad, frame_rows.reshape(1, 2 * count, chan)


def solution(mesh):
    in_specs = (P("dp", "ctx", None), P(), P(), P(), P(), P(), P("dp", "ctx", None))
    out_specs = (P("ctx", "dp"), P("dp", "ctx", None))
    dp_size, ctx_size = mesh.shape["dp"], mesh.shape["ctx"]

    def plan(frames, *others):
        count, chan = frames.shape[1] // 2, frames.shape[2]
        share = 3 * chan // ctx_size
        fits = count == HEAD_DIM and ctx_size % 2 == 0 and ctx_size * count <= 512
        if fits and chan % (128 * dp_size) == 0 and share == 192 and dp_size % 2 == 0:
            return local_fused(dp_size, ctx_size, frames, *others)
        return local(frames, *others)

    return jax.shard_map(plan, mesh=mesh, in_specs=in_specs, out_specs=out_specs, check_vma=False)
```

```python
import functools
import math

import jax
import jax.numpy as jnp
from jax import lax
from jax.experimental import pallas as pl
from jax.experimental.pallas import tpu as pltpu
from jax.sharding import PartitionSpec as P

HEADS = 6
HEAD_DIM = 64


SQRT_HALF = 0.7071067811865476
INV_ROOT_TAU = 0.3989422804014327
EPSILON = 1e-05


def from_behind(value, axis, steps):
    count = lax.axis_size(axis)
    initial, last = (max(0, -steps), min(count, count - steps))
    return lax.ppermute(value, axis, [(source, source + steps) for source in range(initial, last)])


def gelu_slope(pre):
    return 0.5 * (1.0 + lax.erf(pre * SQRT_HALF)) + pre * INV_ROOT_TAU * jnp.exp(-0.5 * pre * pre)


def blocked(step_fn, carry, piece):
    rows = piece[0].shape[0]
    block_rows = math.gcd(rows, 512)
    block_count = rows // block_rows
    stacked = tuple(
        (member.reshape((block_count, block_rows) + member.shape[1:]) for member in piece)
    )

    def inner(state, item):
        block_index, members = item
        return (step_fn(state, members, block_index * block_rows), None)

    final, unused = lax.scan(inner, carry, (jnp.arange(block_count, dtype=jnp.int32), stacked))
    return final


def local(frames, conv_weight, proj_weight, query_weight, key_weight, value_weight, cotangent):
    inputs = frames[0]
    count = inputs.shape[0] // 2
    width = inputs.shape[1]
    following = from_behind(inputs[:1], "ctx", -1)
    paired = inputs.reshape(count, 2, width)
    tap_first = paired[:, 0]
    tap_second = paired[:, 1]
    tap_third = jnp.concatenate([tap_first[1:], following], 0)
    conv_out = jnp.dot(tap_first, conv_weight[0], preferred_element_type=jnp.float32)
    conv_out = conv_out + jnp.dot(tap_second, conv_weight[1], preferred_element_type=jnp.float32)
    conv_out = conv_out + jnp.dot(tap_third, conv_weight[2], preferred_element_type=jnp.float32)
    activated = jax.nn.gelu(conv_out, approximate=False)
    centre = jnp.mean(activated, -1, keepdims=True)
    spread = jnp.mean((activated - centre) ** 2, -1, keepdims=True)
    inv_std = lax.rsqrt(spread + EPSILON)
    normed = (activated - centre) * inv_std
    hidden = jnp.dot(
        normed.astype(jnp.bfloat16), proj_weight, preferred_element_type=jnp.float32
    ).astype(jnp.bfloat16)
    queries = jnp.dot(hidden, query_weight, preferred_element_type=jnp.float32).astype(jnp.bfloat16)
    keys = jnp.dot(hidden, key_weight, preferred_element_type=jnp.float32).astype(jnp.bfloat16)
    values = jnp.dot(hidden, value_weight, preferred_element_type=jnp.float32).astype(jnp.bfloat16)
    upstream = cotangent[0]
    scale = HEAD_DIM ** (-0.5)
    query_heads = queries.reshape(count, HEADS, HEAD_DIM)
    key_heads = keys.reshape(count, HEADS, HEAD_DIM)
    value_heads = values.reshape(count, HEADS, HEAD_DIM)
    grad_heads = upstream.reshape(count, HEADS, HEAD_DIM)

    def forward_block(carry, piece, start):
        running_top, running_total, accum = carry
        rows = piece[0].shape[0]
        keys_part = piece[0].reshape(rows, HEADS, HEAD_DIM)
        values_part = piece[1].reshape(rows, HEADS, HEAD_DIM)
        scores = (
            jnp.einsum("qhe,khe->hqk", query_heads, keys_part, preferred_element_type=jnp.float32)
            * scale
        )
        new_top = jnp.maximum(running_top, jnp.max(scores, -1))
        factor = jnp.exp(running_top - new_top)
        weights = jnp.exp(scores - new_top[:, :, None])
        new_total = running_total * factor + jnp.sum(weights, -1)
        new_accum = accum * jnp.transpose(factor)[:, :, None] + jnp.einsum(
            "hqk,khe->qhe",
            weights,
            values_part.astype(jnp.float32),
            precision=lax.Precision.HIGHEST,
        )
        return (new_top, new_total, new_accum)

    start_state = (
        jnp.full((HEADS, count), -jnp.inf, jnp.float32),
        jnp.zeros((HEADS, count), jnp.float32),
        jnp.zeros((count, HEADS, HEAD_DIM), jnp.float32),
    )
    final_top, final_total, final_accum = blocked(
        forward_block,
        start_state,
        (
            lax.all_gather(keys, "ctx", axis=0, tiled=True),
            lax.all_gather(values, "ctx", axis=0, tiled=True),
        ),
    )
    lse_heads = final_top + jnp.log(final_total)
    outputs = final_accum / jnp.transpose(final_total)[:, :, None]
    delta_rows = jnp.sum(grad_heads.astype(jnp.float32) * outputs, -1)
    delta_heads = jnp.transpose(delta_rows)

    def query_block(carry, piece, start):
        rows = piece[0].shape[0]
        keys_part = piece[0].reshape(rows, HEADS, HEAD_DIM)
        values_part = piece[1].reshape(rows, HEADS, HEAD_DIM)
        scores = (
            jnp.einsum("qhe,khe->hqk", query_heads, keys_part, preferred_element_type=jnp.float32)
            * scale
        )
        probs = jnp.exp(scores - lse_heads[:, :, None])
        prob_grad = jnp.einsum(
            "qhe,khe->hqk", grad_heads, values_part, preferred_element_type=jnp.float32
        )
        score_grad = probs * (prob_grad - delta_heads[:, :, None])
        return carry + jnp.einsum(
            "hqk,khe->qhe",
            score_grad.astype(jnp.bfloat16),
            keys_part,
            preferred_element_type=jnp.float32,
        )

    query_start = jnp.zeros((count, HEADS, HEAD_DIM), jnp.float32)
    query_accum = blocked(
        query_block,
        query_start,
        (
            lax.all_gather(keys, "ctx", axis=0, tiled=True),
            lax.all_gather(values, "ctx", axis=0, tiled=True),
        ),
    )
    query_grad = (query_accum * scale).astype(jnp.bfloat16).reshape(count, HEADS * HEAD_DIM)
    all_lse, all_delta = (
        lax.all_gather(jnp.transpose(lse_heads), "ctx", axis=0, tiled=True),
        lax.all_gather(delta_rows, "ctx", axis=0, tiled=True),
    )

    def key_block(carry, piece, start):
        key_accum, value_accum = carry
        rows = piece[0].shape[0]
        query_part = piece[0].reshape(rows, HEADS, HEAD_DIM)
        grad_part = piece[1].reshape(rows, HEADS, HEAD_DIM)
        lse_part = jnp.transpose(lax.dynamic_slice_in_dim(all_lse, start, rows, 0))
        delta_part = jnp.transpose(lax.dynamic_slice_in_dim(all_delta, start, rows, 0))
        scores = (
            jnp.einsum("qhe,khe->hqk", query_part, key_heads, preferred_element_type=jnp.float32)
            * scale
        )
        probs = jnp.exp(scores - lse_part[:, :, None])
        value_accum = value_accum + jnp.einsum(
            "hqk,qhe->khe",
            probs.astype(jnp.bfloat16),
            grad_part,
            preferred_element_type=jnp.float32,
        )
        prob_grad = jnp.einsum(
            "qhe,khe->hqk", grad_part, value_heads, preferred_element_type=jnp.float32
        )
        score_grad = probs * (prob_grad - delta_part[:, :, None])
        key_accum = key_accum + jnp.einsum(
            "hqk,qhe->khe",
            score_grad.astype(jnp.bfloat16),
            query_part,
            preferred_element_type=jnp.float32,
        )
        return (key_accum, value_accum)

    key_start = (
        jnp.zeros((count, HEADS, HEAD_DIM), jnp.float32),
        jnp.zeros((count, HEADS, HEAD_DIM), jnp.float32),
    )
    key_accum, value_accum = blocked(
        key_block,
        key_start,
        (
            lax.all_gather(queries, "ctx", axis=0, tiled=True),
            lax.all_gather(upstream, "ctx", axis=0, tiled=True),
        ),
    )
    key_grad = (key_accum * scale).astype(jnp.bfloat16).reshape(count, HEADS * HEAD_DIM)
    value_grad = value_accum.astype(jnp.bfloat16).reshape(count, HEADS * HEAD_DIM)
    hidden_grad = jnp.einsum(
        "tk,dk->td", query_grad, query_weight, preferred_element_type=jnp.float32
    )
    hidden_grad = hidden_grad + jnp.einsum(
        "tk,dk->td", key_grad, key_weight, preferred_element_type=jnp.float32
    )
    hidden_grad = hidden_grad + jnp.einsum(
        "tk,dk->td", value_grad, value_weight, preferred_element_type=jnp.float32
    )
    hidden_grad = hidden_grad.astype(jnp.bfloat16)
    normed_grad = jnp.einsum(
        "td,cd->tc", hidden_grad, proj_weight, preferred_element_type=jnp.float32
    )
    act_grad = inv_std * (
        normed_grad
        - jnp.mean(normed_grad, -1, keepdims=True)
        - normed * jnp.mean(normed_grad * normed, -1, keepdims=True)
    )
    conv_grad = (act_grad * gelu_slope(conv_out)).astype(jnp.bfloat16)
    kernel_terms = jnp.concatenate(
        [
            jnp.einsum("tc,to->co", tap_first, conv_grad, preferred_element_type=jnp.float32),
            jnp.einsum("tc,to->co", tap_second, conv_grad, preferred_element_type=jnp.float32),
            jnp.einsum("tc,to->co", tap_third, conv_grad, preferred_element_type=jnp.float32),
        ],
        0,
    )
    earlier = from_behind(conv_grad[count - 1 :], "ctx", 1)
    first = jnp.einsum("to,co->tc", conv_grad, conv_weight[0], preferred_element_type=jnp.float32)
    second = jnp.einsum("to,co->tc", conv_grad, conv_weight[1], preferred_element_type=jnp.float32)
    third = jnp.einsum("to,co->tc", conv_grad, conv_weight[2], preferred_element_type=jnp.float32)
    incoming = jnp.einsum("to,co->tc", earlier, conv_weight[2], preferred_element_type=jnp.float32)
    moved = jnp.concatenate([incoming, third[:-1]], 0)
    even_rows = first + moved
    frame_rows = jnp.stack([even_rows, second], 1).reshape(2 * count, width).astype(jnp.bfloat16)
    frame_sum = lax.psum_scatter(
        kernel_terms.astype(jnp.bfloat16), "ctx", scatter_dimension=0, tiled=True
    )
    weight_grad = lax.psum_scatter(frame_sum, "dp", scatter_dimension=1, tiled=True).astype(
        jnp.float32
    )
    return (weight_grad, frame_rows[None])


MESH = pl.DeviceIdType.MESH
ROW_ROW = (((1,), (1,)), ((), ()))
COL_COL = (((0,), (0,)), ((), ()))
PAIR = 2 * HEAD_DIM
GROUP = 2


def product(left, right, dims=(((1,), (0,)), ((), ()))):
    return lax.dot_general(left, right, dims, preferred_element_type=jnp.float32)


def normalised(conv_out):
    activated = 0.5 * conv_out * (1.0 + lax.erf(conv_out * SQRT_HALF))
    centre = jnp.mean(activated, -1, keepdims=True)
    spread = jnp.mean((activated - centre) ** 2, -1, keepdims=True)
    inv_std = lax.rsqrt(spread + EPSILON)
    return (activated - centre) * inv_std, inv_std


def fused(
    dp_size, ctx_size, count,
    frames, upstream, conv_hbm, proj_hbm, query_hbm, key_hbm, value_hbm,
    weight_out, frame_out,
    taps, cots, conv_w, proj_w, query_w, key_w, value_w,
    conv_all, q_all, k_all, v_all, stats, grads, cgs, window, z_send, z_recv,
    load_sem, frame_send, frame_recv, cot_send, cot_recv, stat_send, stat_recv,
    cg_send, cg_recv, zs_sem, zr_sem,
):
    me = lax.axis_index("ctx")
    record = lax.axis_index("dp")
    chips = ctx_size // 2
    chip, core = me // 2, me % 2
    sibling = chip * 2 + (1 - core)
    width = frames.shape[1]
    chan = width // 2
    total = ctx_size * count
    own = pl.ds(pl.multiple_of(me * count, count), count)

    def rows_of(index):
        return pl.ds(pl.multiple_of(index * count, count), count)

    def peer(step):
        return lax.rem(chip + step, chips) * 2 + core

    loads = []
    for slot, (source, target) in enumerate(
        [
            (frames, taps.at[own, pl.ds(0, width)]),
            (conv_hbm, conv_w),
            (proj_hbm, proj_w),
            (query_hbm, query_w),
            (key_hbm, key_w),
            (value_hbm, value_w),
            (upstream, cots.at[own]),
        ]
    ):
        load = pltpu.make_async_copy(source, target, load_sem.at[slot])
        load.start()
        loads.append(load)

    barrier = pltpu.get_barrier_semaphore()
    for step in range(1, ctx_size):
        pl.semaphore_signal(
            barrier, inc=1, device_id=(record, lax.rem(me + step, ctx_size)), device_id_type=MESH
        )
    for step in range(1, dp_size):
        pl.semaphore_signal(
            barrier, inc=1, device_id=(lax.rem(record + step, dp_size), me), device_id_type=MESH
        )
    pl.semaphore_wait(barrier, ctx_size - 1 + dp_size - 1)

    def transfer(view, send, recv, index, target, slot):
        return pltpu.make_async_remote_copy(
            src_ref=view(index),
            dst_ref=view(index),
            send_sem=send.at[slot],
            recv_sem=recv.at[index],
            device_id=(record, target),
            device_id_type=MESH,
        )

    def scatter(view, send, recv):
        copies = []
        for step in range(1, chips):
            copies.append(transfer(view, send, recv, me, peer(chips - step), step))
        copies.append(transfer(view, send, recv, me, sibling, 0))
        for copy in copies:
            copy.start()
        return copies

    def pass_on(view, send, recv, copies, step):
        source = peer(step)
        copy = transfer(view, send, recv, source, sibling, chips - 1 + step)
        copy.wait_recv()
        copy.start()
        copies.append(copy)

    def arrive(view, send, recv, step):
        source = lax.rem(chip + step, chips) * 2 + (1 - core)
        transfer(view, send, recv, source, sibling, 0).wait_recv()

    def collect(view, send, recv, copies):
        for step in range(1, chips):
            pass_on(view, send, recv, copies, step)
        for step in range(chips):
            arrive(view, send, recv, step)

    def finish(copies):
        for copy in copies:
            copy.wait_send()

    def frame_view(index):
        return taps.at[rows_of(index), pl.ds(0, width)]

    def cot_view(index):
        return cots.at[rows_of(index)]

    def cg_view(half):
        return lambda index: cgs.at[rows_of(index), pl.ds(half * (chan // 2), chan // 2)]

    loads[0].wait()
    frame_copies = scatter(frame_view, frame_send, frame_recv)
    pair_rows = 2 * count
    last_row = lax.broadcasted_iota(jnp.int32, (pair_rows, chan), 0) == pair_rows - 1

    def pair_span(index):
        return pl.ds(pl.multiple_of(index * pair_rows, pair_rows), pair_rows)

    def forward(steps):
        spans = []
        for step in steps:
            here = lax.rem(chip + step, chips)
            after = lax.rem(here + 1, chips)
            span = pair_span(here)
            even = taps[span, 0:chan].astype(jnp.float32)
            head = taps[pl.ds(pl.multiple_of(after * pair_rows, 16), 16), 0:chan]
            following = jnp.where(here < chips - 1, head.astype(jnp.float32)[0:1, :], 0.0)
            taps[span, width : width + chan] = jnp.where(
                last_row, following, pltpu.roll(even, pair_rows - 1, 0)
            ).astype(jnp.bfloat16)
            spans.append(span)
        block = jnp.concatenate([taps[span, :] for span in spans], 0)
        conv_out = product(block, conv_w[...])
        normed = normalised(conv_out)[0]
        hidden = product(normed.astype(jnp.bfloat16), proj_w[...]).astype(jnp.bfloat16)
        queries = product(hidden, query_w[...]).astype(jnp.bfloat16)
        keys = product(hidden, key_w[...]).astype(jnp.bfloat16)
        values = product(hidden, value_w[...]).astype(jnp.bfloat16)
        for place, span in enumerate(spans):
            piece = slice(place * pair_rows, (place + 1) * pair_rows)
            conv_all[span, :] = conv_out[piece]
            q_all[span, :] = queries[piece]
            k_all[span, :] = keys[piece]
            v_all[span, :] = values[piece]

    for load in loads[1:6]:
        load.wait()
    arrive(frame_view, frame_send, frame_recv, 0)
    waiting = []
    for step in range(1, chips + 2):
        if step < chips:
            pass_on(frame_view, frame_send, frame_recv, frame_copies, step)
        if 1 < step <= chips:
            arrive(frame_view, frame_send, frame_recv, step - 1)
        if step > 1:
            waiting.append(step - 2)
        if step == chips - 1:
            loads[6].wait()
            cot_copies = scatter(cot_view, cot_send, cot_recv)
        if len(waiting) == GROUP or (waiting and step == chips + 1):
            forward(waiting)
            waiting = []

    scale = HEAD_DIM ** (-0.5)
    lanes = lax.broadcasted_iota(jnp.int32, (count, PAIR), 1)
    low = (lanes < HEAD_DIM).astype(jnp.float32).astype(jnp.bfloat16)
    high = (lanes >= HEAD_DIM).astype(jnp.float32).astype(jnp.bfloat16)

    def spread_pair(block):
        return jnp.concatenate([block * low, block * high], 0)

    def join_pair(square):
        return jnp.where(lanes < HEAD_DIM, square[:count], square[count:])

    pairs = HEADS // 2
    features = HEADS * HEAD_DIM
    stats[me] = jnp.zeros(stats.shape[1:], jnp.float32)
    saved = []
    for pair in range(pairs):
        cols = slice(pair * PAIR, (pair + 1) * PAIR)
        scores = product(k_all[:, cols], spread_pair(q_all[own, cols]), ROW_ROW) * scale
        prob_grad = product(v_all[:, cols], spread_pair(cots[own, cols]), ROW_ROW)
        top = jnp.max(scores, 0, keepdims=True)
        weights = jnp.exp(scores - top)
        mass = jnp.sum(weights, 0, keepdims=True)
        probs = weights / mass
        delta = jnp.sum(probs * prob_grad, 0, keepdims=True)
        stats[me, pair : pair + 1, :] = top + jnp.log(mass)
        stats[me, 4 + pair : 5 + pair, :] = delta
        saved.append((probs * (prob_grad - delta)).astype(jnp.bfloat16))
    stat_copies = []
    for step in range(1, ctx_size):
        copy = pltpu.make_async_remote_copy(
            src_ref=stats.at[me],
            dst_ref=stats.at[me],
            send_sem=stat_send.at[step],
            recv_sem=stat_recv.at[me],
            device_id=(record, lax.rem(me + step, ctx_size)),
            device_id_type=MESH,
        )
        copy.start()
        stat_copies.append(copy)
    for pair in range(pairs):
        cols = slice(pair * PAIR, (pair + 1) * PAIR)
        square = product(saved[pair], k_all[:, cols], COL_COL)
        grads[:, cols] = (join_pair(square) * scale).astype(jnp.bfloat16)
    collect(cot_view, cot_send, cot_recv, cot_copies)
    first_products = []
    for pair in range(pairs):
        cols = slice(pair * PAIR, (pair + 1) * PAIR)
        first_products.append(
            (
                product(spread_pair(k_all[own, cols]), q_all[:, cols], ROW_ROW) * scale,
                product(spread_pair(v_all[own, cols]), cots[:, cols], ROW_ROW),
            )
        )
    for step in range(1, ctx_size):
        source = lax.rem(me + step, ctx_size)
        pltpu.make_async_remote_copy(
            src_ref=stats.at[source],
            dst_ref=stats.at[source],
            send_sem=stat_send.at[step],
            recv_sem=stat_recv.at[source],
            device_id=(record, source),
            device_id_type=MESH,
        ).wait_recv()

    def along(row):
        halves = []
        for start in (0, HEAD_DIM):
            line = jnp.concatenate(
                [stats[index, row : row + 1, start : start + count] for index in range(ctx_size)], 1
            )
            halves.append(jnp.broadcast_to(line, (count, total)))
        return jnp.concatenate(halves, 0)

    for pair in range(pairs):
        cols = slice(pair * PAIR, (pair + 1) * PAIR)
        scores, prob_grad = first_products[pair]
        probs = jnp.exp(scores - along(pair))
        value_square = product(probs.astype(jnp.bfloat16), cots[:, cols])
        score_grad = (probs * (prob_grad - along(4 + pair))).astype(jnp.bfloat16)
        key_square = product(score_grad, q_all[:, cols])
        at_key = features + pair * PAIR
        at_value = 2 * features + pair * PAIR
        grads[:, at_key : at_key + PAIR] = (join_pair(key_square) * scale).astype(jnp.bfloat16)
        grads[:, at_value : at_value + PAIR] = join_pair(value_square).astype(jnp.bfloat16)

    hidden_grad = product(grads[:, 0:features], query_w[...], ROW_ROW)
    hidden_grad += product(grads[:, features : 2 * features], key_w[...], ROW_ROW)
    hidden_grad += product(grads[:, 2 * features : 3 * features], value_w[...], ROW_ROW)
    normed_grad = product(hidden_grad.astype(jnp.bfloat16), proj_w[...], ROW_ROW)
    conv_out = conv_all[own, :]
    normed, inv_std = normalised(conv_out)
    act_grad = inv_std * (
        normed_grad
        - jnp.mean(normed_grad, -1, keepdims=True)
        - normed * jnp.mean(normed_grad * normed, -1, keepdims=True)
    )
    conv_grad = (act_grad * gelu_slope(conv_out)).astype(jnp.bfloat16)
    cgs[own, :] = conv_grad
    cg_parts = [
        scatter(cg_view(half), cg_send.at[half], cg_recv.at[half]) for half in range(2)
    ]
    frame_out[:, chan:width] = product(
        conv_grad, conv_w[chan : 2 * chan, :], ROW_ROW
    ).astype(jnp.bfloat16)
    even_rows = product(conv_grad, conv_w[0:chan, :], ROW_ROW)
    share = weight_out.shape[0]
    columns = weight_out.shape[1]
    base = (me * share) // 128 * 128
    shift = pl.multiple_of(me * share - base, 64)
    picked = taps[:, pl.ds(pl.multiple_of(base, 128), 256)]

    def z_copy(index):
        return pltpu.make_async_remote_copy(
            src_ref=z_send.at[index],
            dst_ref=z_recv.at[record],
            send_sem=zs_sem.at[index],
            recv_sem=zr_sem.at[record],
            device_id=(index, me),
            device_id_type=MESH,
        )

    for half in range(2):
        collect(cg_view(half), cg_send.at[half], cg_recv.at[half], cg_parts[half])
        side = slice(half * (chan // 2), (half + 1) * (chan // 2))
        window[:, side] = product(picked, cgs[:, side], COL_COL)
        for index in range(half * dp_size // 2, (half + 1) * dp_size // 2):
            z_send[index] = window[
                pl.ds(shift, share), index * columns : (index + 1) * columns
            ].astype(jnp.bfloat16)

            @pl.when(record != index)
            def _():
                z_copy(index).start()

    before = lax.rem(me + ctx_size - 1, ctx_size)
    tail = cgs[pl.ds(pl.multiple_of(before * count + count - 16, 16), 16), :].astype(jnp.float32)
    incoming = jnp.where(me > 0, tail[15:16, :], 0.0)
    first_row = lax.broadcasted_iota(jnp.int32, (count, chan), 0) == 0
    moved = pltpu.roll(cgs[own, :].astype(jnp.float32), 1, 0)
    moved = jnp.where(first_row, incoming, moved).astype(jnp.bfloat16)
    even_rows = even_rows + product(moved, conv_w[2 * chan : 3 * chan, :], ROW_ROW)
    frame_out[:, 0:chan] = even_rows.astype(jnp.bfloat16)

    result = z_send[record].astype(jnp.float32)
    for step in range(1, dp_size):
        source = lax.rem(record + step, dp_size)
        pltpu.make_async_remote_copy(
            src_ref=z_recv.at[source],
            dst_ref=z_recv.at[source],
            send_sem=zs_sem.at[source],
            recv_sem=zr_sem.at[source],
            device_id=(source, me),
            device_id_type=MESH,
        ).wait_recv()
        result = result + z_recv[source].astype(jnp.float32)
    weight_out[...] = result
    for copies in (frame_copies, cot_copies, stat_copies, cg_parts[0], cg_parts[1]):
        finish(copies)
    for index in range(dp_size):

        @pl.when(record != index)
        def _():
            z_copy(index).wait_send()


def local_fused(
    dp_size, ctx_size,
    frames, conv_weight, proj_weight, query_weight, key_weight, value_weight, cotangent,
):
    inputs = frames[0]
    count, chan = inputs.shape[0] // 2, inputs.shape[1]
    total = ctx_size * count
    depth, features = query_weight.shape
    share, columns = 3 * chan // ctx_size, chan // dp_size
    half = jnp.bfloat16
    dma = pltpu.SemaphoreType.DMA
    weight_grad, frame_rows = pl.pallas_call(
        functools.partial(fused, dp_size, ctx_size, count),
        out_shape=(
            jax.ShapeDtypeStruct((share, columns), jnp.float32),
            jax.ShapeDtypeStruct((count, 2 * chan), half),
        ),
        in_specs=[pl.BlockSpec(memory_space=pltpu.HBM)] * 7,
        out_specs=[pl.BlockSpec(memory_space=pltpu.VMEM)] * 2,
        scratch_shapes=[
            pltpu.VMEM((total, 3 * chan), half),
            pltpu.VMEM((total, features), half),
            pltpu.VMEM((3 * chan, chan), half),
            pltpu.VMEM((chan, depth), half),
            pltpu.VMEM((depth, features), half),
            pltpu.VMEM((depth, features), half),
            pltpu.VMEM((depth, features), half),
            pltpu.VMEM((total, chan), jnp.float32),
            pltpu.VMEM((total, features), half),
            pltpu.VMEM((total, features), half),
            pltpu.VMEM((total, features), half),
            pltpu.VMEM((ctx_size, 8, PAIR), jnp.float32),
            pltpu.VMEM((count, 3 * features), half),
            pltpu.VMEM((total, chan), half),
            pltpu.VMEM((256, chan), jnp.float32),
            pltpu.VMEM((dp_size, share, columns), half),
            pltpu.VMEM((dp_size, share, columns), half),
            dma((7,)),
            dma((ctx_size,)),
            dma((ctx_size,)),
            dma((ctx_size,)),
            dma((ctx_size,)),
            dma((ctx_size,)),
            dma((ctx_size,)),
            dma((2, ctx_size)),
            dma((2, ctx_size)),
            dma((dp_size,)),
            dma((dp_size,)),
        ],
        compiler_params=pltpu.CompilerParams(
            collective_id=0, has_side_effects=True, vmem_limit_bytes=60 * 2**20
        ),
    )(
        inputs.reshape(count, 2 * chan),
        cotangent[0],
        conv_weight.reshape(3 * chan, chan),
        proj_weight,
        query_weight,
        key_weight,
        value_weight,
    )
    return weight_grad, frame_rows.reshape(1, 2 * count, chan)


def solution(mesh):
    in_specs = (P("dp", "ctx", None), P(), P(), P(), P(), P(), P("dp", "ctx", None))
    out_specs = (P("ctx", "dp"), P("dp", "ctx", None))
    dp_size, ctx_size = mesh.shape["dp"], mesh.shape["ctx"]

    def plan(frames, *others):
        count, chan = frames.shape[1] // 2, frames.shape[2]
        share = 3 * chan // ctx_size
        fits = count == HEAD_DIM and ctx_size % 2 == 0 and ctx_size > 2 and ctx_size * count <= 512
        if fits and chan % (128 * dp_size) == 0 and share == 192 and dp_size % 2 == 0:
            return local_fused(dp_size, ctx_size, frames, *others)
        return local(frames, *others)

    return jax.shard_map(plan, mesh=mesh, in_specs=in_specs, out_specs=out_specs, check_vma=False)
```

```python
import functools
import math

import jax
import jax.numpy as jnp
from jax import lax
from jax.experimental import pallas as pl
from jax.experimental.pallas import tpu as pltpu
from jax.sharding import PartitionSpec as P

HEADS = 6
HEAD_DIM = 64


SQRT_HALF = 0.7071067811865476
INV_ROOT_TAU = 0.3989422804014327
EPSILON = 1e-05


def from_behind(value, axis, steps):
    count = lax.axis_size(axis)
    initial, last = (max(0, -steps), min(count, count - steps))
    return lax.ppermute(value, axis, [(source, source + steps) for source in range(initial, last)])


def gelu_slope(pre):
    return 0.5 * (1.0 + lax.erf(pre * SQRT_HALF)) + pre * INV_ROOT_TAU * jnp.exp(-0.5 * pre * pre)


def blocked(step_fn, carry, piece):
    rows = piece[0].shape[0]
    block_rows = math.gcd(rows, 512)
    block_count = rows // block_rows
    stacked = tuple(
        (member.reshape((block_count, block_rows) + member.shape[1:]) for member in piece)
    )

    def inner(state, item):
        block_index, members = item
        return (step_fn(state, members, block_index * block_rows), None)

    final, unused = lax.scan(inner, carry, (jnp.arange(block_count, dtype=jnp.int32), stacked))
    return final


def local(frames, conv_weight, proj_weight, query_weight, key_weight, value_weight, cotangent):
    inputs = frames[0]
    count = inputs.shape[0] // 2
    width = inputs.shape[1]
    following = from_behind(inputs[:1], "ctx", -1)
    paired = inputs.reshape(count, 2, width)
    tap_first = paired[:, 0]
    tap_second = paired[:, 1]
    tap_third = jnp.concatenate([tap_first[1:], following], 0)
    conv_out = jnp.dot(tap_first, conv_weight[0], preferred_element_type=jnp.float32)
    conv_out = conv_out + jnp.dot(tap_second, conv_weight[1], preferred_element_type=jnp.float32)
    conv_out = conv_out + jnp.dot(tap_third, conv_weight[2], preferred_element_type=jnp.float32)
    activated = jax.nn.gelu(conv_out, approximate=False)
    centre = jnp.mean(activated, -1, keepdims=True)
    spread = jnp.mean((activated - centre) ** 2, -1, keepdims=True)
    inv_std = lax.rsqrt(spread + EPSILON)
    normed = (activated - centre) * inv_std
    hidden = jnp.dot(
        normed.astype(jnp.bfloat16), proj_weight, preferred_element_type=jnp.float32
    ).astype(jnp.bfloat16)
    queries = jnp.dot(hidden, query_weight, preferred_element_type=jnp.float32).astype(jnp.bfloat16)
    keys = jnp.dot(hidden, key_weight, preferred_element_type=jnp.float32).astype(jnp.bfloat16)
    values = jnp.dot(hidden, value_weight, preferred_element_type=jnp.float32).astype(jnp.bfloat16)
    upstream = cotangent[0]
    scale = HEAD_DIM ** (-0.5)
    query_heads = queries.reshape(count, HEADS, HEAD_DIM)
    key_heads = keys.reshape(count, HEADS, HEAD_DIM)
    value_heads = values.reshape(count, HEADS, HEAD_DIM)
    grad_heads = upstream.reshape(count, HEADS, HEAD_DIM)

    def forward_block(carry, piece, start):
        running_top, running_total, accum = carry
        rows = piece[0].shape[0]
        keys_part = piece[0].reshape(rows, HEADS, HEAD_DIM)
        values_part = piece[1].reshape(rows, HEADS, HEAD_DIM)
        scores = (
            jnp.einsum("qhe,khe->hqk", query_heads, keys_part, preferred_element_type=jnp.float32)
            * scale
        )
        new_top = jnp.maximum(running_top, jnp.max(scores, -1))
        factor = jnp.exp(running_top - new_top)
        weights = jnp.exp(scores - new_top[:, :, None])
        new_total = running_total * factor + jnp.sum(weights, -1)
        new_accum = accum * jnp.transpose(factor)[:, :, None] + jnp.einsum(
            "hqk,khe->qhe",
            weights,
            values_part.astype(jnp.float32),
            precision=lax.Precision.HIGHEST,
        )
        return (new_top, new_total, new_accum)

    start_state = (
        jnp.full((HEADS, count), -jnp.inf, jnp.float32),
        jnp.zeros((HEADS, count), jnp.float32),
        jnp.zeros((count, HEADS, HEAD_DIM), jnp.float32),
    )
    final_top, final_total, final_accum = blocked(
        forward_block,
        start_state,
        (
            lax.all_gather(keys, "ctx", axis=0, tiled=True),
            lax.all_gather(values, "ctx", axis=0, tiled=True),
        ),
    )
    lse_heads = final_top + jnp.log(final_total)
    outputs = final_accum / jnp.transpose(final_total)[:, :, None]
    delta_rows = jnp.sum(grad_heads.astype(jnp.float32) * outputs, -1)
    delta_heads = jnp.transpose(delta_rows)

    def query_block(carry, piece, start):
        rows = piece[0].shape[0]
        keys_part = piece[0].reshape(rows, HEADS, HEAD_DIM)
        values_part = piece[1].reshape(rows, HEADS, HEAD_DIM)
        scores = (
            jnp.einsum("qhe,khe->hqk", query_heads, keys_part, preferred_element_type=jnp.float32)
            * scale
        )
        probs = jnp.exp(scores - lse_heads[:, :, None])
        prob_grad = jnp.einsum(
            "qhe,khe->hqk", grad_heads, values_part, preferred_element_type=jnp.float32
        )
        score_grad = probs * (prob_grad - delta_heads[:, :, None])
        return carry + jnp.einsum(
            "hqk,khe->qhe",
            score_grad.astype(jnp.bfloat16),
            keys_part,
            preferred_element_type=jnp.float32,
        )

    query_start = jnp.zeros((count, HEADS, HEAD_DIM), jnp.float32)
    query_accum = blocked(
        query_block,
        query_start,
        (
            lax.all_gather(keys, "ctx", axis=0, tiled=True),
            lax.all_gather(values, "ctx", axis=0, tiled=True),
        ),
    )
    query_grad = (query_accum * scale).astype(jnp.bfloat16).reshape(count, HEADS * HEAD_DIM)
    all_lse, all_delta = (
        lax.all_gather(jnp.transpose(lse_heads), "ctx", axis=0, tiled=True),
        lax.all_gather(delta_rows, "ctx", axis=0, tiled=True),
    )

    def key_block(carry, piece, start):
        key_accum, value_accum = carry
        rows = piece[0].shape[0]
        query_part = piece[0].reshape(rows, HEADS, HEAD_DIM)
        grad_part = piece[1].reshape(rows, HEADS, HEAD_DIM)
        lse_part = jnp.transpose(lax.dynamic_slice_in_dim(all_lse, start, rows, 0))
        delta_part = jnp.transpose(lax.dynamic_slice_in_dim(all_delta, start, rows, 0))
        scores = (
            jnp.einsum("qhe,khe->hqk", query_part, key_heads, preferred_element_type=jnp.float32)
            * scale
        )
        probs = jnp.exp(scores - lse_part[:, :, None])
        value_accum = value_accum + jnp.einsum(
            "hqk,qhe->khe",
            probs.astype(jnp.bfloat16),
            grad_part,
            preferred_element_type=jnp.float32,
        )
        prob_grad = jnp.einsum(
            "qhe,khe->hqk", grad_part, value_heads, preferred_element_type=jnp.float32
        )
        score_grad = probs * (prob_grad - delta_part[:, :, None])
        key_accum = key_accum + jnp.einsum(
            "hqk,qhe->khe",
            score_grad.astype(jnp.bfloat16),
            query_part,
            preferred_element_type=jnp.float32,
        )
        return (key_accum, value_accum)

    key_start = (
        jnp.zeros((count, HEADS, HEAD_DIM), jnp.float32),
        jnp.zeros((count, HEADS, HEAD_DIM), jnp.float32),
    )
    key_accum, value_accum = blocked(
        key_block,
        key_start,
        (
            lax.all_gather(queries, "ctx", axis=0, tiled=True),
            lax.all_gather(upstream, "ctx", axis=0, tiled=True),
        ),
    )
    key_grad = (key_accum * scale).astype(jnp.bfloat16).reshape(count, HEADS * HEAD_DIM)
    value_grad = value_accum.astype(jnp.bfloat16).reshape(count, HEADS * HEAD_DIM)
    hidden_grad = jnp.einsum(
        "tk,dk->td", query_grad, query_weight, preferred_element_type=jnp.float32
    )
    hidden_grad = hidden_grad + jnp.einsum(
        "tk,dk->td", key_grad, key_weight, preferred_element_type=jnp.float32
    )
    hidden_grad = hidden_grad + jnp.einsum(
        "tk,dk->td", value_grad, value_weight, preferred_element_type=jnp.float32
    )
    hidden_grad = hidden_grad.astype(jnp.bfloat16)
    normed_grad = jnp.einsum(
        "td,cd->tc", hidden_grad, proj_weight, preferred_element_type=jnp.float32
    )
    act_grad = inv_std * (
        normed_grad
        - jnp.mean(normed_grad, -1, keepdims=True)
        - normed * jnp.mean(normed_grad * normed, -1, keepdims=True)
    )
    conv_grad = (act_grad * gelu_slope(conv_out)).astype(jnp.bfloat16)
    kernel_terms = jnp.concatenate(
        [
            jnp.einsum("tc,to->co", tap_first, conv_grad, preferred_element_type=jnp.float32),
            jnp.einsum("tc,to->co", tap_second, conv_grad, preferred_element_type=jnp.float32),
            jnp.einsum("tc,to->co", tap_third, conv_grad, preferred_element_type=jnp.float32),
        ],
        0,
    )
    earlier = from_behind(conv_grad[count - 1 :], "ctx", 1)
    first = jnp.einsum("to,co->tc", conv_grad, conv_weight[0], preferred_element_type=jnp.float32)
    second = jnp.einsum("to,co->tc", conv_grad, conv_weight[1], preferred_element_type=jnp.float32)
    third = jnp.einsum("to,co->tc", conv_grad, conv_weight[2], preferred_element_type=jnp.float32)
    incoming = jnp.einsum("to,co->tc", earlier, conv_weight[2], preferred_element_type=jnp.float32)
    moved = jnp.concatenate([incoming, third[:-1]], 0)
    even_rows = first + moved
    frame_rows = jnp.stack([even_rows, second], 1).reshape(2 * count, width).astype(jnp.bfloat16)
    frame_sum = lax.psum_scatter(
        kernel_terms.astype(jnp.bfloat16), "ctx", scatter_dimension=0, tiled=True
    )
    weight_grad = lax.psum_scatter(frame_sum, "dp", scatter_dimension=1, tiled=True).astype(
        jnp.float32
    )
    return (weight_grad, frame_rows[None])


MESH = pl.DeviceIdType.MESH
ROW_ROW = (((1,), (1,)), ((), ()))
COL_COL = (((0,), (0,)), ((), ()))
PAIR = 2 * HEAD_DIM
GROUP = 1


def product(left, right, dims=(((1,), (0,)), ((), ()))):
    return lax.dot_general(left, right, dims, preferred_element_type=jnp.float32)


def normalised(conv_out):
    activated = 0.5 * conv_out * (1.0 + lax.erf(conv_out * SQRT_HALF))
    centre = jnp.mean(activated, -1, keepdims=True)
    spread = jnp.mean((activated - centre) ** 2, -1, keepdims=True)
    inv_std = lax.rsqrt(spread + EPSILON)
    return (activated - centre) * inv_std, inv_std


def fused(
    dp_size, ctx_size, count,
    frames, upstream, conv_hbm, proj_hbm, query_hbm, key_hbm, value_hbm,
    weight_out, frame_out,
    taps, cots, conv_w, proj_w, query_w, key_w, value_w,
    conv_all, q_all, k_all, v_all, stats, grads, cgs, window, z_send, z_recv,
    load_sem, frame_send, frame_recv, cot_send, cot_recv, stat_send, stat_recv,
    cg_send, cg_recv, zs_sem, zr_sem,
):
    me = lax.axis_index("ctx")
    record = lax.axis_index("dp")
    chips = ctx_size // 2
    chip, core = me // 2, me % 2
    sibling = chip * 2 + (1 - core)
    width = frames.shape[1]
    chan = width // 2
    total = ctx_size * count
    own = pl.ds(pl.multiple_of(me * count, count), count)

    def rows_of(index):
        return pl.ds(pl.multiple_of(index * count, count), count)

    def peer(step):
        return lax.rem(chip + step, chips) * 2 + core

    loads = []
    for slot, (source, target) in enumerate(
        [
            (frames, taps.at[own, pl.ds(0, width)]),
            (conv_hbm, conv_w),
            (proj_hbm, proj_w),
            (query_hbm, query_w),
            (key_hbm, key_w),
            (value_hbm, value_w),
            (upstream, cots.at[own]),
        ]
    ):
        load = pltpu.make_async_copy(source, target, load_sem.at[slot])
        load.start()
        loads.append(load)

    barrier = pltpu.get_barrier_semaphore()
    for step in range(1, ctx_size):
        pl.semaphore_signal(
            barrier, inc=1, device_id=(record, lax.rem(me + step, ctx_size)), device_id_type=MESH
        )
    for step in range(1, dp_size):
        pl.semaphore_signal(
            barrier, inc=1, device_id=(lax.rem(record + step, dp_size), me), device_id_type=MESH
        )
    pl.semaphore_wait(barrier, ctx_size - 1 + dp_size - 1)

    def transfer(view, send, recv, index, target, slot):
        return pltpu.make_async_remote_copy(
            src_ref=view(index),
            dst_ref=view(index),
            send_sem=send.at[slot],
            recv_sem=recv.at[index],
            device_id=(record, target),
            device_id_type=MESH,
        )

    def scatter(view, send, recv):
        copies = []
        for step in range(1, chips):
            copies.append(transfer(view, send, recv, me, peer(chips - step), step))
        copies.append(transfer(view, send, recv, me, sibling, 0))
        for copy in copies:
            copy.start()
        return copies

    def pass_on(view, send, recv, copies, step):
        source = peer(step)
        copy = transfer(view, send, recv, source, sibling, chips - 1 + step)
        copy.wait_recv()
        copy.start()
        copies.append(copy)

    def arrive(view, send, recv, step):
        source = lax.rem(chip + step, chips) * 2 + (1 - core)
        transfer(view, send, recv, source, sibling, 0).wait_recv()

    def collect(view, send, recv, copies):
        for step in range(1, chips):
            pass_on(view, send, recv, copies, step)
        for step in range(chips):
            arrive(view, send, recv, step)

    def finish(copies):
        for copy in copies:
            copy.wait_send()

    def frame_view(index):
        return taps.at[rows_of(index), pl.ds(0, width)]

    def cot_view(index):
        return cots.at[rows_of(index)]

    def cg_view(half):
        return lambda index: cgs.at[rows_of(index), pl.ds(half * (chan // 2), chan // 2)]

    loads[0].wait()
    frame_copies = scatter(frame_view, frame_send, frame_recv)
    pair_rows = 2 * count
    last_row = lax.broadcasted_iota(jnp.int32, (pair_rows, chan), 0) == pair_rows - 1

    def pair_span(index):
        return pl.ds(pl.multiple_of(index * pair_rows, pair_rows), pair_rows)

    def forward(steps):
        spans = []
        for step in steps:
            here = lax.rem(chip + step, chips)
            after = lax.rem(here + 1, chips)
            span = pair_span(here)
            even = taps[span, 0:chan].astype(jnp.float32)
            head = taps[pl.ds(pl.multiple_of(after * pair_rows, 16), 16), 0:chan]
            following = jnp.where(here < chips - 1, head.astype(jnp.float32)[0:1, :], 0.0)
            taps[span, width : width + chan] = jnp.where(
                last_row, following, pltpu.roll(even, pair_rows - 1, 0)
            ).astype(jnp.bfloat16)
            spans.append(span)
        block = jnp.concatenate([taps[span, :] for span in spans], 0)
        conv_out = product(block, conv_w[...])
        normed = normalised(conv_out)[0]
        hidden = product(normed.astype(jnp.bfloat16), proj_w[...]).astype(jnp.bfloat16)
        queries = product(hidden, query_w[...]).astype(jnp.bfloat16)
        keys = product(hidden, key_w[...]).astype(jnp.bfloat16)
        values = product(hidden, value_w[...]).astype(jnp.bfloat16)
        for place, span in enumerate(spans):
            piece = slice(place * pair_rows, (place + 1) * pair_rows)
            conv_all[span, :] = conv_out[piece]
            q_all[span, :] = queries[piece]
            k_all[span, :] = keys[piece]
            v_all[span, :] = values[piece]

    for load in loads[1:6]:
        load.wait()
    arrive(frame_view, frame_send, frame_recv, 0)
    waiting = []
    for step in range(1, chips + 2):
        if step < chips:
            pass_on(frame_view, frame_send, frame_recv, frame_copies, step)
        if 1 < step <= chips:
            arrive(frame_view, frame_send, frame_recv, step - 1)
        if step > 1:
            waiting.append(step - 2)
        if step == chips - 1:
            loads[6].wait()
            cot_copies = scatter(cot_view, cot_send, cot_recv)
        if len(waiting) == GROUP or (waiting and step == chips + 1):
            forward(waiting)
            waiting = []

    scale = HEAD_DIM ** (-0.5)
    lanes = lax.broadcasted_iota(jnp.int32, (count, PAIR), 1)
    low = (lanes < HEAD_DIM).astype(jnp.float32).astype(jnp.bfloat16)
    high = (lanes >= HEAD_DIM).astype(jnp.float32).astype(jnp.bfloat16)

    def spread_pair(block):
        return jnp.concatenate([block * low, block * high], 0)

    def join_pair(square):
        return jnp.where(lanes < HEAD_DIM, square[:count], square[count:])

    pairs = HEADS // 2
    features = HEADS * HEAD_DIM
    stats[me] = jnp.zeros(stats.shape[1:], jnp.float32)
    saved = []
    for pair in range(pairs):
        cols = slice(pair * PAIR, (pair + 1) * PAIR)
        scores = product(k_all[:, cols], spread_pair(q_all[own, cols]), ROW_ROW) * scale
        prob_grad = product(v_all[:, cols], spread_pair(cots[own, cols]), ROW_ROW)
        top = jnp.max(scores, 0, keepdims=True)
        weights = jnp.exp(scores - top)
        mass = jnp.sum(weights, 0, keepdims=True)
        probs = weights / mass
        delta = jnp.sum(probs * prob_grad, 0, keepdims=True)
        stats[me, pair : pair + 1, :] = top + jnp.log(mass)
        stats[me, 4 + pair : 5 + pair, :] = delta
        saved.append((probs * (prob_grad - delta)).astype(jnp.bfloat16))
    stat_copies = []
    for step in range(1, ctx_size):
        copy = pltpu.make_async_remote_copy(
            src_ref=stats.at[me],
            dst_ref=stats.at[me],
            send_sem=stat_send.at[step],
            recv_sem=stat_recv.at[me],
            device_id=(record, lax.rem(me + step, ctx_size)),
            device_id_type=MESH,
        )
        copy.start()
        stat_copies.append(copy)
    for pair in range(pairs):
        cols = slice(pair * PAIR, (pair + 1) * PAIR)
        square = product(saved[pair], k_all[:, cols], COL_COL)
        grads[:, cols] = (join_pair(square) * scale).astype(jnp.bfloat16)
    collect(cot_view, cot_send, cot_recv, cot_copies)
    first_products = []
    for pair in range(pairs):
        cols = slice(pair * PAIR, (pair + 1) * PAIR)
        first_products.append(
            (
                product(spread_pair(k_all[own, cols]), q_all[:, cols], ROW_ROW) * scale,
                product(spread_pair(v_all[own, cols]), cots[:, cols], ROW_ROW),
            )
        )
    for step in range(1, ctx_size):
        source = lax.rem(me + step, ctx_size)
        pltpu.make_async_remote_copy(
            src_ref=stats.at[source],
            dst_ref=stats.at[source],
            send_sem=stat_send.at[step],
            recv_sem=stat_recv.at[source],
            device_id=(record, source),
            device_id_type=MESH,
        ).wait_recv()

    def along(row):
        halves = []
        for start in (0, HEAD_DIM):
            line = jnp.concatenate(
                [stats[index, row : row + 1, start : start + count] for index in range(ctx_size)], 1
            )
            halves.append(jnp.broadcast_to(line, (count, total)))
        return jnp.concatenate(halves, 0)

    for pair in range(pairs):
        cols = slice(pair * PAIR, (pair + 1) * PAIR)
        scores, prob_grad = first_products[pair]
        probs = jnp.exp(scores - along(pair))
        value_square = product(probs.astype(jnp.bfloat16), cots[:, cols])
        score_grad = (probs * (prob_grad - along(4 + pair))).astype(jnp.bfloat16)
        key_square = product(score_grad, q_all[:, cols])
        at_key = features + pair * PAIR
        at_value = 2 * features + pair * PAIR
        grads[:, at_key : at_key + PAIR] = (join_pair(key_square) * scale).astype(jnp.bfloat16)
        grads[:, at_value : at_value + PAIR] = join_pair(value_square).astype(jnp.bfloat16)

    hidden_grad = product(grads[:, 0:features], query_w[...], ROW_ROW)
    hidden_grad += product(grads[:, features : 2 * features], key_w[...], ROW_ROW)
    hidden_grad += product(grads[:, 2 * features : 3 * features], value_w[...], ROW_ROW)
    normed_grad = product(hidden_grad.astype(jnp.bfloat16), proj_w[...], ROW_ROW)
    conv_out = conv_all[own, :]
    normed, inv_std = normalised(conv_out)
    act_grad = inv_std * (
        normed_grad
        - jnp.mean(normed_grad, -1, keepdims=True)
        - normed * jnp.mean(normed_grad * normed, -1, keepdims=True)
    )
    conv_grad = (act_grad * gelu_slope(conv_out)).astype(jnp.bfloat16)
    cgs[own, :] = conv_grad
    cg_parts = [
        scatter(cg_view(half), cg_send.at[half], cg_recv.at[half]) for half in range(2)
    ]
    frame_out[:, chan:width] = product(
        conv_grad, conv_w[chan : 2 * chan, :], ROW_ROW
    ).astype(jnp.bfloat16)
    share = weight_out.shape[0]
    columns = weight_out.shape[1]
    base = (me * share) // 128 * 128
    shift = pl.multiple_of(me * share - base, 64)
    picked = taps[:, pl.ds(pl.multiple_of(base, 128), 256)]

    def z_copy(index):
        return pltpu.make_async_remote_copy(
            src_ref=z_send.at[index],
            dst_ref=z_recv.at[record],
            send_sem=zs_sem.at[index],
            recv_sem=zr_sem.at[record],
            device_id=(index, me),
            device_id_type=MESH,
        )

    for half in range(2):
        collect(cg_view(half), cg_send.at[half], cg_recv.at[half], cg_parts[half])
        side = slice(half * (chan // 2), (half + 1) * (chan // 2))
        window[:, side] = product(picked, cgs[:, side], COL_COL)
        for index in range(half * dp_size // 2, (half + 1) * dp_size // 2):
            z_send[index] = window[
                pl.ds(shift, share), index * columns : (index + 1) * columns
            ].astype(jnp.bfloat16)

            @pl.when(record != index)
            def _():
                z_copy(index).start()

    before = lax.rem(me + ctx_size - 1, ctx_size)
    tail = cgs[pl.ds(pl.multiple_of(before * count + count - 16, 16), 16), :].astype(jnp.float32)
    incoming = jnp.where(me > 0, tail[15:16, :], 0.0)
    first_row = lax.broadcasted_iota(jnp.int32, (count, chan), 0) == 0
    moved = pltpu.roll(cgs[own, :].astype(jnp.float32), 1, 0)
    moved = jnp.where(first_row, incoming, moved).astype(jnp.bfloat16)
    even_rows = product(conv_grad, conv_w[0:chan, :], ROW_ROW)
    even_rows = even_rows + product(moved, conv_w[2 * chan : 3 * chan, :], ROW_ROW)
    frame_out[:, 0:chan] = even_rows.astype(jnp.bfloat16)

    result = z_send[record].astype(jnp.float32)
    for step in range(1, dp_size):
        source = lax.rem(record + step, dp_size)
        pltpu.make_async_remote_copy(
            src_ref=z_recv.at[source],
            dst_ref=z_recv.at[source],
            send_sem=zs_sem.at[source],
            recv_sem=zr_sem.at[source],
            device_id=(source, me),
            device_id_type=MESH,
        ).wait_recv()
        result = result + z_recv[source].astype(jnp.float32)
    weight_out[...] = result
    for copies in (frame_copies, cot_copies, stat_copies, cg_parts[0], cg_parts[1]):
        finish(copies)
    for index in range(dp_size):

        @pl.when(record != index)
        def _():
            z_copy(index).wait_send()


def local_fused(
    dp_size, ctx_size,
    frames, conv_weight, proj_weight, query_weight, key_weight, value_weight, cotangent,
):
    inputs = frames[0]
    count, chan = inputs.shape[0] // 2, inputs.shape[1]
    total = ctx_size * count
    depth, features = query_weight.shape
    share, columns = 3 * chan // ctx_size, chan // dp_size
    half = jnp.bfloat16
    dma = pltpu.SemaphoreType.DMA
    weight_grad, frame_rows = pl.pallas_call(
        functools.partial(fused, dp_size, ctx_size, count),
        out_shape=(
            jax.ShapeDtypeStruct((share, columns), jnp.float32),
            jax.ShapeDtypeStruct((count, 2 * chan), half),
        ),
        in_specs=[pl.BlockSpec(memory_space=pltpu.HBM)] * 7,
        out_specs=[pl.BlockSpec(memory_space=pltpu.VMEM)] * 2,
        scratch_shapes=[
            pltpu.VMEM((total, 3 * chan), half),
            pltpu.VMEM((total, features), half),
            pltpu.VMEM((3 * chan, chan), half),
            pltpu.VMEM((chan, depth), half),
            pltpu.VMEM((depth, features), half),
            pltpu.VMEM((depth, features), half),
            pltpu.VMEM((depth, features), half),
            pltpu.VMEM((total, chan), jnp.float32),
            pltpu.VMEM((total, features), half),
            pltpu.VMEM((total, features), half),
            pltpu.VMEM((total, features), half),
            pltpu.VMEM((ctx_size, 8, PAIR), jnp.float32),
            pltpu.VMEM((count, 3 * features), half),
            pltpu.VMEM((total, chan), half),
            pltpu.VMEM((256, chan), jnp.float32),
            pltpu.VMEM((dp_size, share, columns), half),
            pltpu.VMEM((dp_size, share, columns), half),
            dma((7,)),
            dma((ctx_size,)),
            dma((ctx_size,)),
            dma((ctx_size,)),
            dma((ctx_size,)),
            dma((ctx_size,)),
            dma((ctx_size,)),
            dma((2, ctx_size)),
            dma((2, ctx_size)),
            dma((dp_size,)),
            dma((dp_size,)),
        ],
        compiler_params=pltpu.CompilerParams(
            collective_id=0, has_side_effects=True, vmem_limit_bytes=60 * 2**20
        ),
    )(
        inputs.reshape(count, 2 * chan),
        cotangent[0],
        conv_weight.reshape(3 * chan, chan),
        proj_weight,
        query_weight,
        key_weight,
        value_weight,
    )
    return weight_grad, frame_rows.reshape(1, 2 * count, chan)


def solution(mesh):
    in_specs = (P("dp", "ctx", None), P(), P(), P(), P(), P(), P("dp", "ctx", None))
    out_specs = (P("ctx", "dp"), P("dp", "ctx", None))
    dp_size, ctx_size = mesh.shape["dp"], mesh.shape["ctx"]

    def plan(frames, *others):
        count, chan = frames.shape[1] // 2, frames.shape[2]
        share = 3 * chan // ctx_size
        fits = count == HEAD_DIM and ctx_size % 2 == 0 and ctx_size > 2 and ctx_size * count <= 512
        if fits and chan % (128 * dp_size) == 0 and share == 192 and dp_size % 2 == 0:
            return local_fused(dp_size, ctx_size, frames, *others)
        return local(frames, *others)

    return jax.shard_map(plan, mesh=mesh, in_specs=in_specs, out_specs=out_specs, check_vma=False)
```
